256 devices in a mesh: seq: 32 (over z, y_lo, core), comp: 8 (over x, y_hi).
Axes of the slice: x: 4, y: 4 (y_hi: 2, y_lo: 2; y = y_hi * 2 + y_lo), z: 8, core: 2. Of those that a mesh axis runs over, the one named last changes fastest.
Arguments:
- prompt_inputs: bfloat16 [16384, 128, 64], P('seq', 'comp'), may hold values from -1.25 to 1.25
- prompt_keys: bfloat16 [16384, 8, 128], P('seq', 'comp'), may hold values from -1.75 to 1.75
- prompt_queries: bfloat16 [16384, 8, 128], P('seq', 'comp'), may hold values from -1.75 to 1.75
- prompt_logdecay: float32 [16384, 128], P('seq', 'comp'), may hold values from -1 to 0, as said below
- prompt_cotangent: bfloat16 [16384, 128, 64], P('seq', 'comp'), may hold values from -0.125 to 0.125
- answer_inputs: bfloat16 [8, 1024, 128, 64], P('comp', None, 'seq'), may hold values from -1.25 to 1.25
- answer_keys: bfloat16 [8, 1024, 8, 128], P('comp'), may hold values from -1.75 to 1.75
- answer_queries: bfloat16 [8, 1024, 8, 128], P('comp'), may hold values from -1.75 to 1.75
- answer_logdecay: float32 [8, 1024, 128], P('comp', None, 'seq'), may hold values from -1 to 0, as said below
- answer_cotangent: bfloat16 [8, 1024, 128, 64], P('comp', None, 'seq'), may hold values from -0.125 to 0.125
- answer_lengths: int32 [8], P('comp'), may hold values from 256 to 1024, as said below
Outputs:
- prompt_inputgrad: bfloat16 [16384, 128, 64], P('seq', 'comp')
- prompt_keygrad: bfloat16 [16384, 8, 128], P('seq', 'comp')
- prompt_querygrad: bfloat16 [16384, 8, 128], P('seq', 'comp')
- answer_inputgrad: bfloat16 [8, 1024, 128, 64], P('comp', None, 'seq')
- answer_keygrad: bfloat16 [8, 1024, 8, 128], P('comp', 'seq')
- answer_querygrad: bfloat16 [8, 1024, 8, 128], P('comp', 'seq')
The draws below stay inside these ranges and needn't reach their ends.
Inputs may be any that keep to these rules, and one draw needn't show every extreme that they name: `answer_lengths`: live tokens of each answer, counted from its start. `prompt_logdecay`: negative log decay factors. `answer_logdecay`: negative log decay factors.
All inputs are finite; a program needn't handle non-finite values.
Results may differ from the reference program's by a relative error of at most 0.0014.
Values sent between devices are 32-bit elements; how exact they have to be, the bound alone decides.
No kernel may reach another device: no remote copies, remote signals or barrier semaphores. Data moves between devices by JAX's collectives and lax.ppermute only.
A program may use at most 128 MiB of HBM per device.

```python
import math
import jax
import jax.numpy as jnp
from jax import lax

HEAD_SUBSET = 128
HEAD_DIM = 64
STATE = 128
GROUPS = 8
BLOCK = 256
PROMPT_DEV = 512
ANSWER_LEN = 1024
PROMPT = 16384
ANSWERS = 8


def head_speed(key, fast_share):
    return jax.random.uniform(jax.random.fold_in(key, 101), (HEAD_SUBSET,)) < fast_share


def head_rates(key):
    rate_key = jax.random.fold_in(key, 202)
    slow_key, quick_key = jax.random.split(rate_key)
    gradual_rate = jax.random.uniform(slow_key, (HEAD_SUBSET,), minval=0.05, maxval=0.2) * math.log(10.0) / PROMPT
    quick_rate = 1.0 / jax.random.uniform(quick_key, (HEAD_SUBSET,), minval=30.0, maxval=50.0)
    return (gradual_rate, quick_rate)


def decay_lookup(key, total_rows, rows_per_block, spike_fraction, gradual_rate, quick_rate, quick_heads):
    every_key_row = jax.random.split(key, 4)
    baseline_rate = jnp.where(quick_heads, quick_rate, gradual_rate)
    block_multiplier = jnp.exp(jax.random.uniform(every_key_row[0], (total_rows // rows_per_block, HEAD_SUBSET), minval=math.log(0.5), maxval=math.log(2.0)))
    block_multiplier = jnp.repeat(block_multiplier, rows_per_block, axis=0)
    jitter_amount = jax.random.uniform(every_key_row[1], (total_rows, HEAD_SUBSET), minval=0.5, maxval=1.5)
    spike_events = jax.random.uniform(every_key_row[2], (total_rows, HEAD_SUBSET)) < spike_fraction
    sudden_falls = jnp.log(jax.random.uniform(every_key_row[3], (total_rows, HEAD_SUBSET), minval=0.6, maxval=0.8))
    return -baseline_rate[None, :] * block_multiplier * jitter_amount + jnp.where(spike_events, sudden_falls, 0.0)


def draw_prompt_logdecay(key, part):
    quick_heads = head_speed(key, 0.5)
    gradual_rate, quick_rate = head_rates(key)
    key = jax.random.fold_in(key, 11)
    return decay_lookup(key, PROMPT, PROMPT_DEV, 2.0 / PROMPT, gradual_rate, quick_rate, quick_heads).astype(jnp.float32)


def draw_answer_logdecay(key, part):
    quick_heads = head_speed(key, 0.5)
    gradual_rate, quick_rate = head_rates(key)
    key = jax.random.fold_in(key, 13)
    table = decay_lookup(key, ANSWERS * ANSWER_LEN, ANSWER_LEN, 2.0 / ANSWER_LEN, gradual_rate, quick_rate, quick_heads)
    return table.reshape(ANSWERS, ANSWER_LEN, HEAD_SUBSET).astype(jnp.float32)


def draw_answer_lengths(key, part):
    key = jax.random.fold_in(key, 23)
    length_key, order_key = jax.random.split(key)
    drawn_lengths = jax.random.randint(length_key, (ANSWERS,), ANSWER_LEN // 4, ANSWER_LEN + 1)
    shuffle = jax.random.permutation(order_key, ANSWERS)
    drawn_lengths = drawn_lengths.at[shuffle[0]].set(ANSWER_LEN)
    drawn_lengths = drawn_lengths.at[shuffle[1]].set(ANSWER_LEN // 4)
    return drawn_lengths.astype(jnp.int32)


def block_scale(own_key, extent, cuts, low, largest):
    loudness = 1.0
    for dim, blocks in cuts:
        steps = jax.random.uniform(jax.random.fold_in(jax.random.fold_in(own_key, 6), dim), (blocks,), jnp.float32, low / len(cuts), largest / len(cuts))
        loudness = loudness * jnp.repeat(jnp.exp(steps), extent[dim] // blocks).reshape((-1,) + (1,) * (len(extent) - 1 - dim))
    return loudness


def normal_values(own_key, shape, spread, reach, shards=(), held_as=jnp.bfloat16):
    factor_of = block_scale(own_key, shape, shards, -0.22, 0.18) if shards else 1.0
    drawn = jax.random.normal(own_key, shape, jnp.float32) * spread * factor_of
    return jnp.minimum(jnp.maximum(drawn, -reach), reach).astype(held_as)


def setup_inputs(seed: int = 0) -> dict:
    arg_keys = jax.random.split(jax.random.key(seed), 12)
    prompt_inputs = normal_values(arg_keys[0], (PROMPT, HEAD_SUBSET, HEAD_DIM), 0.2, 1.25, ((0, 32), (1, 8)))
    prompt_keys = normal_values(arg_keys[1], (PROMPT, GROUPS, STATE), 0.3, 1.75, ((0, 32), (1, 8)))
    prompt_queries = normal_values(arg_keys[2], (PROMPT, GROUPS, STATE), 0.3, 1.75, ((0, 32), (1, 8)))
    prompt_logdecay = draw_prompt_logdecay(jax.random.fold_in(arg_keys[11], 71), 0)
    prompt_cotangent = normal_values(arg_keys[4], (PROMPT, HEAD_SUBSET, HEAD_DIM), 0.02, 0.125, ((0, 32), (1, 8)))
    answer_inputs = normal_values(arg_keys[5], (ANSWERS, ANSWER_LEN, HEAD_SUBSET, HEAD_DIM), 0.2, 1.25, ((0, 8), (2, 32)))
    answer_keys = normal_values(arg_keys[6], (ANSWERS, ANSWER_LEN, GROUPS, STATE), 0.3, 1.75, ((0, 8),))
    answer_queries = normal_values(arg_keys[7], (ANSWERS, ANSWER_LEN, GROUPS, STATE), 0.3, 1.75, ((0, 8),))
    answer_logdecay = draw_answer_logdecay(jax.random.fold_in(arg_keys[11], 71), 0)
    answer_cotangent = normal_values(arg_keys[9], (ANSWERS, ANSWER_LEN, HEAD_SUBSET, HEAD_DIM), 0.02, 0.125, ((0, 8), (2, 32)))
    answer_lengths = draw_answer_lengths(jax.random.fold_in(arg_keys[11], 71), 0)
    return {"prompt_inputs": prompt_inputs, "prompt_keys": prompt_keys, "prompt_queries": prompt_queries, "prompt_logdecay": prompt_logdecay, "prompt_cotangent": prompt_cotangent, "answer_inputs": answer_inputs, "answer_keys": answer_keys, "answer_queries": answer_queries, "answer_logdecay": answer_logdecay, "answer_cotangent": answer_cotangent, "answer_lengths": answer_lengths}


PRECISE = lax.Precision.HIGHEST

def block_forward(start_state, pieces):
    inputs, key_rows, queries, logdecay = pieces
    length = inputs.shape[0]
    per_group = inputs.shape[1] // key_rows.shape[1]
    keys_head = jnp.repeat(key_rows, per_group, axis=1)
    queries_head = jnp.repeat(queries, per_group, axis=1)
    cumlog = jnp.cumsum(logdecay, axis=0)
    row_ids = lax.broadcasted_iota(jnp.int32, (length, length), 0)
    col_ids = lax.broadcasted_iota(jnp.int32, (length, length), 1)
    causal = (row_ids >= col_ids)[None]
    trail_logs = jnp.transpose(cumlog)
    log_gap = trail_logs[:, :, None] - trail_logs[:, None, :]
    weights = jnp.where(causal, jnp.exp(jnp.where(causal, log_gap, 0.0)), 0.0)
    scores = jnp.einsum('thn,shn->hts', queries_head, keys_head, precision=PRECISE)
    output = jnp.einsum('hts,shp->thp', weights * scores, inputs, precision=PRECISE)
    output = output + jnp.exp(cumlog)[:, :, None] * jnp.einsum('thn,hnp->thp', queries_head, start_state, precision=PRECISE)
    tail_decay = jnp.exp(cumlog[-1][None, :] - cumlog)
    fresh_state = jnp.einsum('shn,shp->hnp', tail_decay[:, :, None] * keys_head, inputs, precision=PRECISE)
    new_state = jnp.exp(cumlog[-1])[:, None, None] * start_state + fresh_state
    return (new_state, output)

def run_sequence(inputs, key_rows, queries, logdecay, start_state):
    token_count, head_count, head_width = inputs.shape
    blocks = token_count // BLOCK
    pieces = (inputs.reshape(blocks, BLOCK, head_count, head_width), key_rows.reshape(blocks, BLOCK, key_rows.shape[1], key_rows.shape[2]), queries.reshape(blocks, BLOCK, queries.shape[1], queries.shape[2]), logdecay.reshape(blocks, BLOCK, head_count))
    final_state, outputs = lax.scan(jax.checkpoint(block_forward), start_state, pieces)
    return (outputs.reshape(token_count, head_count, head_width), final_state)

def reference(prompt_inputs, prompt_keys, prompt_queries, prompt_logdecay, prompt_cotangent, answer_inputs, answer_keys, answer_queries, answer_logdecay, answer_cotangent, answer_lengths):
    live_mask = (lax.broadcasted_iota(jnp.int32, (ANSWERS, ANSWER_LEN), 1) < answer_lengths[:, None]).astype(jnp.float32)
    answer_weight = answer_cotangent.astype(jnp.float32) * live_mask[:, :, None, None]
    prompt_weight = prompt_cotangent.astype(jnp.float32)

    def objective(inputs_prompt, keys_prompt, queries_prompt, inputs_answer, keys_answer, queries_answer):
        zero_state = jnp.zeros((HEAD_SUBSET, STATE, HEAD_DIM), jnp.float32)
        prompt_out, final_state = run_sequence(inputs_prompt, keys_prompt, queries_prompt, prompt_logdecay, zero_state)

        def answer_run(inputs, key_rows, queries, logdecay):
            return run_sequence(inputs, key_rows, queries, logdecay, final_state)[0]
        answer_out = jax.vmap(answer_run)(inputs_answer, keys_answer, queries_answer, answer_logdecay)
        return jnp.sum(prompt_out * prompt_weight) + jnp.sum(answer_out * answer_weight)
    gradients = jax.grad(objective, argnums=(0, 1, 2, 3, 4, 5))(prompt_inputs.astype(jnp.float32), prompt_keys.astype(jnp.float32), prompt_queries.astype(jnp.float32), answer_inputs.astype(jnp.float32), answer_keys.astype(jnp.float32), answer_queries.astype(jnp.float32))
    return (gradients[0].astype(jnp.bfloat16), gradients[1].astype(jnp.bfloat16), gradients[2].astype(jnp.bfloat16), gradients[3].astype(jnp.bfloat16), gradients[4].astype(jnp.bfloat16), gradients[5].astype(jnp.bfloat16))
```

```python
import functools

import jax
import jax.numpy as jnp
from jax import lax
from jax.experimental import pallas as pl
from jax.experimental.pallas import tpu as pltpu
from jax.sharding import PartitionSpec as P

F32 = jnp.float32
BF16 = jnp.bfloat16
T = 128
MID = 63
N = 128
HEAD = 64
VMEM_BYTES = 48 * 1024 * 1024


def dot(left, right):
    return lax.dot_general(left, right, (((1,), (0,)), ((), ())), preferred_element_type=F32)


def dot_nt(left, right):
    return lax.dot_general(left, right, (((1,), (1,)), ((), ())), preferred_element_type=F32)


def split(value):
    high = value.astype(BF16)
    return high, (value - high.astype(F32)).astype(BF16)


def running(logs):
    first, rest = split(logs)
    second, third = split(logs - first.astype(F32))
    upper = lax.broadcasted_iota(jnp.int32, (T, T), 0) <= lax.broadcasted_iota(jnp.int32, (T, T), 1)
    ones = jnp.where(upper, 1.0, 0.0).astype(BF16)
    return dot(first, ones) + (dot(second, ones) + dot(third, ones))


def rows(per_head):
    heads, lanes = per_head.shape
    spread = jnp.broadcast_to(per_head[:, None, :], (heads, HEAD, lanes))
    return spread.reshape(heads * HEAD, lanes)


def column(logs, token):
    return jnp.broadcast_to(logs[:, token : token + 1], logs.shape)


def chunk_logs(logs_ref, number):
    sums = running(logs_ref[:, pl.ds(pl.multiple_of(number * T, T), T)])
    return sums, column(sums, MID), column(sums, T - 1)


def lanes_of(ref, number):
    return ref[:, pl.ds(pl.multiple_of(number * T, T), T)].astype(F32)


def tokens_of(ref, number):
    return ref[pl.ds(pl.multiple_of(number * T, T), T), :]


def live_mask(number, length, width):
    token = lax.broadcasted_iota(jnp.int32, (width, T), 1) + number * T
    return token < length


def twice(value):
    return jnp.concatenate([value, value], axis=0)


def side(left, right):
    return jnp.concatenate([left, right], axis=1)


def ends_kernel(length_ref, cot_ref, logs_ref, query_ref, ends_ref, start_ref):
    chunks, width = ends_ref.shape[0], ends_ref.shape[1]
    start_ref[...] = jnp.zeros_like(start_ref)

    def step(index, carry):
        number = chunks - 1 - index
        sums, mid, last = chunk_logs(logs_ref, number)
        scaled = lanes_of(cot_ref, number) * rows(jnp.exp(sums - mid))
        scaled = jnp.where(live_mask(number, length_ref[0], width), scaled, 0.0)
        high, low = split(scaled)
        pulled = dot(side(high, low), twice(tokens_of(query_ref, number)))
        current = start_ref[...]
        ends_ref[number] = current
        start_ref[...] = rows(jnp.exp(last)) * current + rows(jnp.exp(mid)) * pulled
        return carry

    lax.fori_loop(0, chunks, step, 0)


def summary_kernel(
    input_ref, cot_ref, logs_ref, key_ref, query_ref, carried_ref, pulled_ref, all_c, all_p, total_ref
):
    chunks = carried_ref.shape[0]
    all_c[...] = jnp.zeros_like(all_c)
    all_p[...] = jnp.zeros_like(all_p)
    total_ref[...] = jnp.zeros_like(total_ref)

    def step(number, carry):
        sums, mid, last = chunk_logs(logs_ref, number)
        high, low = split(lanes_of(input_ref, number) * rows(jnp.exp(mid - sums)))
        carried = dot(side(high, low), twice(tokens_of(key_ref, number)))
        carried = rows(jnp.exp(last - mid)) * carried
        carried_ref[number] = carried
        all_c[...] = rows(jnp.exp(last)) * all_c[...] + carried
        high, low = split(lanes_of(cot_ref, number) * rows(jnp.exp(sums - mid)))
        pulled = dot(side(high, low), twice(tokens_of(query_ref, number)))
        pulled = rows(jnp.exp(mid)) * pulled
        pulled_ref[number] = pulled
        all_p[...] = all_p[...] + rows(jnp.exp(total_ref[...])) * pulled
        total_ref[...] = total_ref[...] + last
        return carry

    lax.fori_loop(0, chunks, step, 0)


def scan_kernel(blocks_ref, final_grad_ref, out_ref, final_ref):
    count = blocks_ref.shape[0]
    current = jnp.zeros(final_ref.shape, F32)
    size = current.shape[0]
    for place in range(count):
        out_ref[place, :size] = current
        decay = jnp.exp(blocks_ref[place, 2 * size : 2 * size + 1])
        current = decay * current + blocks_ref[place, :size]
    final_ref[...] = current
    current = final_grad_ref[...]
    for place in range(count - 1, -1, -1):
        out_ref[place, size : 2 * size] = current
        decay = jnp.exp(blocks_ref[place, 2 * size : 2 * size + 1])
        current = decay * current + blocks_ref[place, size : 2 * size]


def chunk_grads(number, inputs, cot, logs3, keys, queries, start, end):
    sums, mid, last = logs3
    grow = rows(jnp.exp(mid - sums))
    fall = rows(jnp.exp(sums - mid))
    in_high, in_low = split(inputs * grow)
    cot_high, cot_low = split(cot * fall)
    end_high, end_low = split(rows(jnp.exp(last - mid)) * end)
    start_high, start_low = split(rows(jnp.exp(mid)) * start)
    first = lax.broadcasted_iota(jnp.int32, (T, T), 0)
    second = lax.broadcasted_iota(jnp.int32, (T, T), 1)
    score_high, score_low = split(jnp.where(first >= second, dot_nt(queries, keys), 0.0))
    input_grad = dot(side(cot_high, cot_low), twice(score_high)) + dot(cot_high, score_low)
    input_grad = input_grad + dot_nt(side(end_high, end_low), side(keys, keys))
    input_grad = grow * input_grad
    in_high_t, in_low_t = in_high.T, in_low.T
    right_high, right_low = side(cot_high, end_high), side(cot_low, end_low)
    both = dot(in_high_t, right_high) + (dot(in_high_t, right_low) + dot(in_low_t, right_high))
    products = jnp.where(second >= first, both[:, :T], 0.0)
    high, low = split(products)
    key_grad = both[:, T:] + dot(side(high, low), twice(queries))
    high, low = split(products.T)
    query_grad = dot(side(high, low), twice(keys))
    cot_high_t, cot_low_t = cot_high.T, cot_low.T
    query_grad = query_grad + dot(cot_high_t, start_high)
    query_grad = query_grad + (dot(cot_high_t, start_low) + dot(cot_low_t, start_high))
    return input_grad, key_grad, query_grad, (in_high, in_low)


def answer_kernel(
    length_ref, input_ref, cot_ref, logs_ref, key_ref, query_ref, ends_ref,
    input_grad_ref, key_grad_ref, query_grad_ref, state_ref,
):
    chunks, width = ends_ref.shape[0], ends_ref.shape[1]
    state_ref[...] = jnp.zeros_like(state_ref)

    def step(number, carry):
        logs3 = chunk_logs(logs_ref, number)
        sums, mid, last = logs3
        cot = jnp.where(live_mask(number, length_ref[0], width), lanes_of(cot_ref, number), 0.0)
        keys, queries = tokens_of(key_ref, number), tokens_of(query_ref, number)
        start = state_ref[...]
        input_grad, key_grad, query_grad, (high, low) = chunk_grads(
            number, lanes_of(input_ref, number), cot, logs3, keys, queries, start, ends_ref[number]
        )
        place = pl.ds(pl.multiple_of(number * T, T), T)
        input_grad_ref[:, place] = input_grad.astype(BF16)
        key_grad_ref[place, :] = key_grad
        query_grad_ref[place, :] = query_grad
        carried = dot(side(high, low), twice(keys))
        state_ref[...] = rows(jnp.exp(last)) * start + rows(jnp.exp(last - mid)) * carried
        return carry

    lax.fori_loop(0, chunks, step, 0)


def prompt_kernel(
    input_ref, cot_ref, logs_ref, key_ref, query_ref, carried_ref, pulled_ref, start_ref, end_ref,
    input_grad_ref, key_grad_ref, query_grad_ref, state_ref, ends_ref,
):
    chunks = carried_ref.shape[0]
    state_ref[...] = end_ref[...]

    def back(index, carry):
        number = chunks - 1 - index
        _, _, last = chunk_logs(logs_ref, number)
        current = state_ref[...]
        ends_ref[number] = current
        state_ref[...] = rows(jnp.exp(last)) * current + pulled_ref[number]
        return carry

    lax.fori_loop(0, chunks, back, 0)
    state_ref[...] = start_ref[...]

    def step(number, carry):
        logs3 = chunk_logs(logs_ref, number)
        keys, queries = tokens_of(key_ref, number), tokens_of(query_ref, number)
        start = state_ref[...]
        input_grad, key_grad, query_grad, _ = chunk_grads(
            number, lanes_of(input_ref, number), lanes_of(cot_ref, number), logs3, keys, queries,
            start, ends_ref[number],
        )
        place = pl.ds(pl.multiple_of(number * T, T), T)
        input_grad_ref[:, place] = input_grad.astype(BF16)
        key_grad_ref[place, :] = key_grad.astype(BF16)
        query_grad_ref[place, :] = query_grad.astype(BF16)
        state_ref[...] = rows(jnp.exp(logs3[2])) * start + carried_ref[number]
        return carry

    lax.fori_loop(0, chunks, step, 0)


def start_part_kernel(length_ref, cot_ref, logs_ref, state_ref, local_ref, out_ref, total_ref):
    chunks, width = out_ref.shape[0] // T, state_ref.shape[0]
    state_high, state_low = split(state_ref[...])
    total_ref[...] = jnp.zeros_like(total_ref)

    def step(number, carry):
        sums, _, last = chunk_logs(logs_ref, number)
        scaled = lanes_of(cot_ref, number) * rows(jnp.exp(total_ref[...] + sums))
        scaled = jnp.where(live_mask(number, length_ref[0], width), scaled, 0.0)
        high, low = split(scaled)
        high, low = high.T, low.T
        part = dot(high, state_high) + (dot(high, state_low) + dot(low, state_high))
        place = pl.ds(pl.multiple_of(number * T, T), T)
        out_ref[place, :] = local_ref[place, :] + part
        total_ref[...] = total_ref[...] + last
        return carry

    lax.fori_loop(0, chunks, step, 0)


def shape(*dims, dtype=F32):
    return jax.ShapeDtypeStruct(dims, dtype)


def call(kernel, outs, scratch=(), scalar=False, count=0, flops=0, name=None):
    vmem = pl.BlockSpec(memory_space=pltpu.VMEM)
    first = [pl.BlockSpec(memory_space=pltpu.SMEM)] if scalar else []
    return pl.pallas_call(
        kernel,
        out_shape=outs,
        in_specs=first + [vmem] * count,
        out_specs=[vmem] * len(outs),
        scratch_shapes=scratch,
        compiler_params=pltpu.CompilerParams(vmem_limit_bytes=VMEM_BYTES),
        cost_estimate=pl.CostEstimate(flops=flops, bytes_accessed=4000000, transcendentals=0),
        name=name,
    )


def body(
    prompt_inputs, prompt_keys, prompt_queries, prompt_logdecay, prompt_cotangent,
    answer_inputs, answer_keys, answer_queries, answer_logdecay, answer_cotangent, answer_lengths,
):
    tokens, heads, _ = prompt_inputs.shape
    _, length, answer_heads, _ = answer_inputs.shape
    width, answer_width = heads * HEAD, answer_heads * HEAD
    chunks, answer_chunks = tokens // T, length // T
    seq, comp = lax.axis_size("seq"), lax.axis_size("comp")
    quads = heads // answer_heads
    planes = seq // quads
    part = answer_width // planes
    swap = [
        ((z * quads + q) * comp + c, (c * quads + q) * comp + z)
        for z in range(planes) for q in range(quads) for c in range(comp)
    ]
    group = lax.axis_index("seq") // quads

    x = jnp.transpose(prompt_inputs, (1, 2, 0)).reshape(width, tokens)
    cot = jnp.transpose(prompt_cotangent, (1, 2, 0)).reshape(width, tokens)
    logs = prompt_logdecay.T
    keys, queries = prompt_keys.reshape(tokens, N), prompt_queries.reshape(tokens, N)
    ax = jnp.transpose(answer_inputs[0], (1, 2, 0)).reshape(answer_width, length)
    acot = jnp.transpose(answer_cotangent[0], (1, 2, 0)).reshape(answer_width, length)
    alogs = answer_logdecay[0].T
    akeys = lax.dynamic_slice_in_dim(answer_keys[0], group, 1, 1).reshape(length, N)
    aqueries = lax.dynamic_slice_in_dim(answer_queries[0], group, 1, 1).reshape(length, N)

    ends, start_grad = call(
        ends_kernel, [shape(answer_chunks, answer_width, N), shape(answer_width, N)],
        scalar=True, count=3, flops=10**9, name="answer_ends",
    )(answer_lengths, acot, alogs, aqueries)
    parts = lax.all_to_all(start_grad.reshape(comp, part, N), "comp", 0, 0, tiled=True)
    final_grad = lax.ppermute(jnp.sum(parts, axis=0), ("seq", "comp"), swap)

    carried, pulled, all_carried, all_pulled, totals = call(
        summary_kernel,
        [shape(chunks, width, N), shape(chunks, width, N), shape(width, N), shape(width, N), shape(heads, N)],
        count=5, flops=10**9, name="prompt_summary",
    )(x, cot, logs, keys, queries)

    ax_grad, ak_grad, aq_local = call(
        answer_kernel,
        [shape(answer_width, length, dtype=BF16), shape(length, N), shape(length, N)],
        scratch=[pltpu.VMEM((answer_width, N), F32)],
        scalar=True, count=6, flops=2 * 10**9, name="answer_grads",
    )(answer_lengths, ax, acot, alogs, akeys, aqueries, ends)

    def by_owner(value):
        value = value.reshape(quads, planes, part, N)
        return jnp.swapaxes(value, 0, 1).reshape(seq, part, N)

    def by_row(value):
        value = value.reshape(planes, quads, part, N)
        return jnp.swapaxes(value, 0, 1).reshape(width, N)

    slice_total = jnp.repeat(totals, HEAD // part, axis=0)[:, None, :]
    slice_total = jnp.broadcast_to(slice_total, (seq, 8, N)).reshape(quads, planes, 8, N)
    slice_total = jnp.swapaxes(slice_total, 0, 1).reshape(seq, 8, N)
    token_part = length // seq
    sent = jnp.concatenate(
        [by_owner(all_carried), by_owner(all_pulled), slice_total, ak_grad.reshape(seq, token_part, N)], axis=1
    )
    got = lax.all_to_all(sent, "seq", 0, 0, tiled=True)
    back, final = call(
        scan_kernel, [shape(seq, 2 * part, N), shape(part, N)], count=2, flops=10**7, name="scan"
    )(got, final_grad)
    key_parts = got[:, 2 * part + 8 :]

    final = lax.ppermute(final, ("seq", "comp"), swap)
    final = lax.all_to_all(jnp.broadcast_to(final[None], (comp, part, N)), "comp", 0, 0, tiled=True)
    (aq_grad,) = call(
        start_part_kernel, [shape(length, N)], scratch=[pltpu.VMEM((answer_heads, N), F32)],
        scalar=True, count=4, flops=10**9, name="answer_start_part",
    )(answer_lengths, acot, alogs, final.reshape(answer_width, N), aq_local)
    sent = jnp.concatenate([back, aq_grad.reshape(seq, token_part, N)], axis=1)
    got = lax.all_to_all(sent, "seq", 0, 0, tiled=True)
    start, end = by_row(got[:, :part]), by_row(got[:, part : 2 * part])
    query_parts = got[:, 2 * part :]

    x_grad, k_grad, q_grad = call(
        prompt_kernel,
        [shape(width, tokens, dtype=BF16), shape(tokens, N, dtype=BF16), shape(tokens, N, dtype=BF16)],
        scratch=[pltpu.VMEM((width, N), F32), pltpu.VMEM((chunks, width, N), F32)],
        count=9, flops=3 * 10**9, name="prompt_grads",
    )(x, cot, logs, keys, queries, carried, pulled, start, end)

    def gather_groups(parts):
        summed = jnp.sum(parts.reshape(planes, quads, token_part, N), axis=1)
        return jnp.swapaxes(summed, 0, 1)[None].astype(BF16)

    return (
        jnp.transpose(x_grad.reshape(heads, HEAD, tokens), (2, 0, 1)),
        k_grad.reshape(tokens, 1, N),
        q_grad.reshape(tokens, 1, N),
        jnp.transpose(ax_grad.reshape(answer_heads, HEAD, length), (2, 0, 1))[None],
        gather_groups(key_parts),
        gather_groups(query_parts),
    )


def solution(mesh):
    in_specs = (
        P("seq", "comp", None),
        P("seq", "comp", None),
        P("seq", "comp", None),
        P("seq", "comp"),
        P("seq", "comp", None),
        P("comp", None, "seq", None),
        P("comp", None, None, None),
        P("comp", None, None, None),
        P("comp", None, "seq"),
        P("comp", None, "seq", None),
        P("comp"),
    )
    out_specs = (
        P("seq", "comp", None),
        P("seq", "comp", None),
        P("seq", "comp", None),
        P("comp", None, "seq", None),
        P("comp", "seq", None, None),
        P("comp", "seq", None, None),
    )
    return jax.shard_map(body, mesh=mesh, in_specs=in_specs, out_specs=out_specs, check_vma=False)
```

```python
import functools

import jax
import jax.numpy as jnp
from jax import lax
from jax.experimental import pallas as pl
from jax.experimental.pallas import tpu as pltpu
from jax.sharding import PartitionSpec as P

F32 = jnp.float32
BF16 = jnp.bfloat16
T = 128
MID = 63
N = 128
GROUPS = 8
HEAD = 64
PART = 32
SMALL, LARGE = 16 * 1024 * 1024, 56 * 1024 * 1024


def dot(left, right):
    return lax.dot_general(left, right, (((1,), (0,)), ((), ())), preferred_element_type=F32)


def dot_nt(left, right):
    return lax.dot_general(left, right, (((1,), (1,)), ((), ())), preferred_element_type=F32)


def split(value):
    high = value.astype(BF16)
    return high, (value - high.astype(F32)).astype(BF16)


def running(logs):
    first, rest = split(logs)
    second, third = split(logs - first.astype(F32))
    upper = lax.broadcasted_iota(jnp.int32, (T, T), 0) <= lax.broadcasted_iota(jnp.int32, (T, T), 1)
    ones = jnp.where(upper, 1.0, 0.0).astype(BF16)
    return dot(first, ones) + (dot(second, ones) + dot(third, ones))


def rows(per_head):
    heads, lanes = per_head.shape
    spread = jnp.broadcast_to(per_head[:, None, :], (heads, HEAD, lanes))
    return spread.reshape(heads * HEAD, lanes)


def column(logs, token):
    return jnp.broadcast_to(logs[:, token : token + 1], logs.shape)


def chunk_logs(logs_ref, number):
    return block_logs(logs_ref[:, number * T : (number + 1) * T])


def block_logs(logs):
    sums = running(logs)
    return sums, column(sums, MID), column(sums, T - 1)


def tokens_of(ref, number):
    return ref[number * T : (number + 1) * T, :]


def lanes_at(ref, number):
    return ref.at[:, number * T : (number + 1) * T]


def tokens_at(ref, number, count=T):
    return ref.at[number * count : (number + 1) * count, :]


def start_copies(pairs, sems, first=0):
    copies = [pltpu.make_async_copy(source, target, sems.at[first + n]) for n, (source, target) in enumerate(pairs)]
    for copy in copies:
        copy.start()
    return copies


def wait_all(copies):
    for copy in copies:
        copy.wait()


def lanes_of(ref, number):
    return ref[:, number * T : (number + 1) * T]


def chunk_pairs(hbm_ref, ref, order):
    return [(hbm_ref.at[n], ref.at[n]) for n in order]


def live_mask(number, length, width):
    token = lax.broadcasted_iota(jnp.int32, (width, T), 1) + number * T
    return token < length


def twice(value):
    return jnp.concatenate([value, value], axis=0)


def side(left, right):
    return jnp.concatenate([left, right], axis=1)


def own_group(ref, group, all_ref):
    all_ref[...] = ref.astype(F32)
    return all_ref[pl.ds(group, T, stride=GROUPS), :].astype(BF16)


def ends_kernel(
    length_ref, group_ref, cot_hbm, logs_hbm, key_hbm, query_hbm, ends_hbm, own_key_hbm, own_query_hbm, start_ref,
    cot_ref, logs_ref, ends_ref, own_key_ref, own_query_ref, raw_k, raw_q, all_k, all_q, sems,
):
    chunks, width = ends_ref.shape[0], ends_ref.shape[1]
    order = list(range(chunks - 1, -1, -1))
    raw_pairs = [(tokens_at(query_hbm, n, T * GROUPS), raw_q.at[n]) for n in order]
    pairs = [(logs_hbm, logs_ref), (cot_hbm, cot_ref)] + raw_pairs
    pairs += [(tokens_at(key_hbm, n, T * GROUPS), raw_k.at[n]) for n in order]
    copies = start_copies(pairs, sems)
    wait_all(copies[:2])
    current = jnp.zeros((width, N), F32)
    sent = []
    for step, n in enumerate(order):
        copies[2 + step].wait()
        queries = own_group(raw_q[n], group_ref[0], all_q.at[step % 2])
        own_query_ref[n * T : (n + 1) * T, :] = queries
        sums, mid, last = chunk_logs(logs_ref, n)
        scaled = lanes_of(cot_ref, n).astype(F32) * rows(jnp.exp(sums - mid))
        scaled = jnp.where(live_mask(n, length_ref[0], width), scaled, 0.0)
        high, low = split(scaled)
        pulled = dot(side(high, low), twice(queries))
        ends_ref[n] = current
        sent += start_copies([(ends_ref.at[n], ends_hbm.at[n])], sems, len(copies) + step)
        current = rows(jnp.exp(last)) * current + rows(jnp.exp(mid)) * pulled
    start_ref[...] = current
    for step, n in enumerate(order):
        copies[2 + chunks + step].wait()
        own_key_ref[n * T : (n + 1) * T, :] = own_group(raw_k[n], group_ref[0], all_k.at[step % 2])
    pairs = [(own_key_ref, own_key_hbm), (own_query_ref, own_query_hbm)]
    wait_all(sent + start_copies(pairs, sems, len(copies) + chunks))


PLANES = 8


def half_rows(place, core):
    return pl.multiple_of((place // PLANES) * 8 * HEAD + core * 4 * HEAD + (place % PLANES) * PART, PART)


def summary_kernel(
    core_ref, input_hbm, cot_hbm, logs_hbm, key_hbm, query_hbm,
    carried_hbm, pulled_hbm, mine_ref, peer_ref, total_ref,
    input_ref, cot_ref, logs_ref, key_ref, query_ref, carried_ref, pulled_ref, all_c, all_p, sems,
):
    chunks = carried_ref.shape[0]
    order = range(chunks)
    pairs = [
        (logs_hbm, logs_ref), (key_hbm, key_ref), (input_hbm, input_ref), (query_hbm, query_ref), (cot_hbm, cot_ref)
    ]
    copies = start_copies(pairs, sems)
    wait_all(copies[:3])
    total = jnp.zeros(total_ref.shape, F32)
    sent = []
    for n in order:
        sums, mid, last = chunk_logs(logs_ref, n)
        high, low = split(lanes_of(input_ref, n).astype(F32) * rows(jnp.exp(mid - sums)))
        carried = dot(side(high, low), twice(tokens_of(key_ref, n)))
        carried = rows(jnp.exp(last - mid)) * carried
        carried_ref[n] = carried
        sent += start_copies([(carried_ref.at[n], carried_hbm.at[n])], sems, len(copies) + 2 * n)
        all_c[...] = carried if n == 0 else rows(jnp.exp(last)) * all_c[...] + carried
        if n == 0:
            wait_all(copies[3:])
        high, low = split(lanes_of(cot_ref, n).astype(F32) * rows(jnp.exp(sums - mid)))
        pulled = dot(side(high, low), twice(tokens_of(query_ref, n)))
        pulled = rows(jnp.exp(mid)) * pulled
        pulled_ref[n] = pulled
        sent += start_copies([(pulled_ref.at[n], pulled_hbm.at[n])], sems, len(copies) + 2 * n + 1)
        all_p[...] = pulled if n == 0 else all_p[...] + rows(jnp.exp(total)) * pulled
        total = total + last
    total_ref[...] = total
    core = core_ref[0]
    places = mine_ref.shape[0]
    for place in range(places):
        for ref, side_core in ((mine_ref, core), (peer_ref, 1 - core)):
            here = pl.ds(half_rows(place, side_core), PART)
            ref[place, :PART] = all_c[here, :]
            ref[place, PART:] = all_p[here, :]
    heads = total_ref.shape[0]
    peer_ref[places, :heads] = total_ref[...]
    peer_ref[places, heads:] = jnp.zeros_like(peer_ref[places, heads:])
    wait_all(sent)


def both_totals(first, head, mine_ref, got_ref):
    mine = mine_ref[pl.ds(head, 1), :]
    theirs = got_ref[got_ref.shape[0] - 1, pl.ds(head, 1), :]
    return jnp.where(first, mine, theirs), jnp.where(first, theirs, mine)


STATES = 2 * PART
GRADS = STATES + 8


def head_of(place, side_y, core):
    return side_y * 8 + core * 4 + place * PART // HEAD


def joined(first, mine, theirs, total0, total1):
    zero, one = jnp.where(first, mine, theirs), jnp.where(first, theirs, mine)
    return jnp.exp(total1) * zero[:PART] + one[:PART], zero[PART:] + jnp.exp(total0) * one[PART:]


def parted(first, mine, theirs, total0, total1, start, end):
    carried0 = jnp.where(first, mine[:PART], theirs[:PART])
    pulled1 = jnp.where(first, theirs[PART:], mine[PART:])
    start1 = jnp.exp(total0) * start + carried0
    end0 = jnp.exp(total1) * end + pulled1
    own = jnp.where(first, start, start1), jnp.where(first, end0, end)
    return own, (jnp.where(first, start1, start), jnp.where(first, end, end0))


def pack_chip_kernel(at_ref, mine_ref, got_ref, total_ref, keep_ref, away_ref, chip_total_ref):
    core, y = at_ref[0], at_ref[1]
    heads = total_ref.shape[0]
    chip_total_ref[...] = total_ref[...] + got_ref[got_ref.shape[0] - 1, :heads]
    for place in range(PLANES):
        for ref, side_y in ((keep_ref, y), (away_ref, 1 - y)):
            total0, total1 = both_totals(core == 0, head_of(place, side_y, core), total_ref, got_ref)
            here = side_y * PLANES + place
            carried, pulled = joined(core == 0, mine_ref[here], got_ref[here], total0, total1)
            ref[place, :PART] = carried
            ref[place, PART:] = pulled
    away_ref[PLANES, :heads] = chip_total_ref[...]
    away_ref[PLANES, heads:] = jnp.zeros_like(away_ref[PLANES, heads:])


def pack_kernel(at_ref, keep_ref, got_ref, total_ref, start_ref, out_ref):
    core, y = at_ref[0], at_ref[1]
    for place in range(PLANES):
        total0, total1 = both_totals(y == 0, head_of(place, y, core), total_ref, got_ref)
        carried, pulled = joined(y == 0, keep_ref[place], got_ref[place], total0, total1)
        out_ref[place, :PART] = carried
        out_ref[place, PART:STATES] = pulled
        out_ref[place, STATES:GRADS] = jnp.broadcast_to(total0 + total1, (8, N))
        out_ref[place, GRADS:] = start_ref[PART * place : PART * (place + 1)]


def scan_kernel(blocks_ref, starts_ref, out_ref):
    current = jnp.zeros((PART, N), F32)
    for place in range(PLANES):
        starts_ref[place] = current
        current = jnp.exp(blocks_ref[place, STATES : STATES + 1]) * current + blocks_ref[place, :PART]
    for group in range(out_ref.shape[0]):
        out_ref[group, :PART] = blocks_ref[group, GRADS:]
        out_ref[group, PART:] = current


def scan_back_kernel(blocks_ref, starts_ref, got_ref, out_ref):
    current = got_ref[0, :PART]
    for answer in range(1, got_ref.shape[0]):
        current = current + got_ref[answer, :PART]
    for place in range(PLANES - 1, -1, -1):
        out_ref[place, :PART] = starts_ref[place]
        out_ref[place, PART:STATES] = current
        out_ref[place, STATES:] = got_ref[place, PART:]
        current = jnp.exp(blocks_ref[place, STATES : STATES + 1]) * current + blocks_ref[place, PART:STATES]


def unpack_kernel(at_ref, keep_ref, got_ref, total_ref, states_ref, own_ref, other_ref):
    core, y = at_ref[0], at_ref[1]
    for place in range(PLANES):
        total0, total1 = both_totals(y == 0, head_of(place, y, core), total_ref, got_ref)
        own, other = parted(
            y == 0, keep_ref[place], got_ref[place], total0, total1,
            states_ref[place, :PART], states_ref[place, PART:STATES],
        )
        for ref, (start, end) in ((own_ref, own), (other_ref, other)):
            ref[place, :PART] = start
            ref[place, PART:] = end


def unpack_chip_kernel(at_ref, mine_ref, got_ref, total_ref, near_ref, away_ref, own_ref, other_ref):
    core, y = at_ref[0], at_ref[1]
    for place in range(PLANES):
        for chip_ref, side_y in ((near_ref, y), (away_ref, 1 - y)):
            total0, total1 = both_totals(core == 0, head_of(place, side_y, core), total_ref, got_ref)
            here = side_y * PLANES + place
            own, other = parted(
                core == 0, mine_ref[here], got_ref[here], total0, total1,
                chip_ref[place, :PART], chip_ref[place, PART:],
            )
            for ref, (start, end) in ((own_ref, own), (other_ref, other)):
                ref[here, :PART] = start
                ref[here, PART:] = end


def gather_kernel(parts_ref, key_ref, query_ref, sums_ref):
    for ref, first in ((key_ref, 0), (query_ref, PART)):
        for group in range(GROUPS):
            chip0, chip1 = parts_ref[2 * group], parts_ref[2 * group + 1]
            sums_ref[pl.ds(group, PART, stride=GROUPS), :] = (chip0 + chip1)[first : first + PART]
        ref[...] = sums_ref[...].astype(BF16)


def chunk_grads(inputs, cot, logs3, keys, queries, start, end):
    sums, mid, last = logs3
    grow = rows(jnp.exp(mid - sums))
    fall = rows(jnp.exp(sums - mid))
    in_high, in_low = split(inputs * grow)
    cot_high, cot_low = split(cot * fall)
    end_high, end_low = split(rows(jnp.exp(last - mid)) * end)
    start_high, start_low = split(rows(jnp.exp(mid)) * start)
    first = lax.broadcasted_iota(jnp.int32, (T, T), 0)
    second = lax.broadcasted_iota(jnp.int32, (T, T), 1)
    score_high, score_low = split(jnp.where(first >= second, dot_nt(queries, keys), 0.0))
    input_grad = dot(side(cot_high, cot_low), twice(score_high)) + dot(cot_high, score_low)
    input_grad = input_grad + dot_nt(side(end_high, end_low), side(keys, keys))
    input_grad = grow * input_grad
    in_high_t, in_low_t = in_high.T, in_low.T
    right_high, right_low = side(cot_high, end_high), side(cot_low, end_low)
    both = dot(in_high_t, right_high) + (dot(in_high_t, right_low) + dot(in_low_t, right_high))
    products = jnp.where(second >= first, both[:, :T], 0.0)
    high, low = split(products)
    key_grad = both[:, T:] + dot(side(high, low), twice(queries))
    high, low = split(products.T)
    query_grad = dot(side(high, low), twice(keys))
    cot_high_t, cot_low_t = cot_high.T, cot_low.T
    query_grad = query_grad + dot(cot_high_t, start_high)
    query_grad = query_grad + (dot(cot_high_t, start_low) + dot(cot_low_t, start_high))
    return input_grad, key_grad, query_grad, (in_high, in_low)


def by_core(number, core, value, mine_ref, peer_ref):
    value = value.reshape(2, 2, PART, N)
    here = pl.ds(2 * number, 2)
    mine_ref[here] = jnp.where(core == 0, value[:, 0], value[:, 1])
    peer_ref[here] = jnp.where(core == 0, value[:, 1], value[:, 0])


def answer_kernel(
    length_ref, core_ref, input_hbm, cot_hbm, logs_hbm, key_hbm, query_hbm, ends_hbm,
    input_grad_hbm, query_grad_hbm, key_mine_ref, key_peer_ref,
    input_ref, cot_ref, logs_ref, key_ref, query_ref, ends_ref, input_grad_ref, query_grad_ref, state_ref, sems,
):
    chunks, width = ends_ref.shape[0], ends_ref.shape[1]
    order = range(chunks)
    pairs = [
        (logs_hbm, logs_ref), (key_hbm, key_ref), (query_hbm, query_ref), (input_hbm, input_ref), (cot_hbm, cot_ref)
    ]
    copies = start_copies(pairs + chunk_pairs(ends_hbm, ends_ref, order), sems)
    wait_all(copies[:5])
    state_ref[...] = jnp.zeros_like(state_ref)
    sent = []
    for n in order:
        logs3 = chunk_logs(logs_ref, n)
        sums, mid, last = logs3
        copies[5 + n].wait()
        cot = jnp.where(live_mask(n, length_ref[0], width), lanes_of(cot_ref, n).astype(F32), 0.0)
        keys, queries = tokens_of(key_ref, n), tokens_of(query_ref, n)
        start = state_ref[...]
        input_grad, key_grad, query_grad, (high, low) = chunk_grads(
            lanes_of(input_ref, n).astype(F32), cot, logs3, keys, queries, start, ends_ref[n]
        )
        input_grad_ref[n] = input_grad.astype(BF16)
        by_core(n, core_ref[0], key_grad, key_mine_ref, key_peer_ref)
        query_grad_ref[n * T : (n + 1) * T, :] = query_grad
        pairs = [
            (input_grad_ref.at[n], lanes_at(input_grad_hbm, n)),
            (tokens_at(query_grad_ref, n), tokens_at(query_grad_hbm, n)),
        ]
        sent += start_copies(pairs, sems, len(copies) + 2 * n)
        carried = dot(side(high, low), twice(keys))
        state_ref[...] = rows(jnp.exp(last)) * start + rows(jnp.exp(last - mid)) * carried
    wait_all(sent)


def prompt_near_kernel(
    input_hbm, cot_hbm, logs_hbm, key_hbm, query_hbm, input_grad_hbm, key_grad_hbm, query_grad_hbm,
    input_ref, cot_ref, logs_ref, key_ref, query_ref, input_grad_ref, key_grad_ref, query_grad_ref, sems,
):
    first = lax.broadcasted_iota(jnp.int32, (T, T), 0)
    second = lax.broadcasted_iota(jnp.int32, (T, T), 1)
    order = range(input_ref.shape[1] // T)
    pairs = [
        (logs_hbm, logs_ref), (key_hbm, key_ref), (query_hbm, query_ref), (input_hbm, input_ref), (cot_hbm, cot_ref)
    ]
    copies = start_copies(pairs, sems)
    wait_all(copies)
    sent = []
    for n in order:
        here = slice(n * T, (n + 1) * T)
        sums, mid, _ = chunk_logs(logs_ref, n)
        keys, queries = tokens_of(key_ref, n), tokens_of(query_ref, n)
        grow = rows(jnp.exp(mid - sums))
        in_high, in_low = split(lanes_of(input_ref, n).astype(F32) * grow)
        cot_high, cot_low = split(lanes_of(cot_ref, n).astype(F32) * rows(jnp.exp(sums - mid)))
        score_high, score_low = split(jnp.where(first >= second, dot_nt(queries, keys), 0.0))
        input_grad = dot(side(cot_high, cot_low), twice(score_high)) + dot(cot_high, score_low)
        input_grad_ref[n] = grow * input_grad
        in_high_t, in_low_t = in_high.T, in_low.T
        both = dot(in_high_t, side(cot_high, cot_low))
        products = both[:, :T] + (both[:, T:] + dot(in_low_t, cot_high))
        products = jnp.where(second >= first, products, 0.0)
        high, low = split(products)
        key_grad_ref[here, :] = dot(side(high, low), twice(queries))
        high, low = split(products.T)
        query_grad_ref[here, :] = dot(side(high, low), twice(keys))
        pairs = [
            (input_grad_ref.at[n], input_grad_hbm.at[n]),
            (tokens_at(key_grad_ref, n), tokens_at(key_grad_hbm, n)),
            (tokens_at(query_grad_ref, n), tokens_at(query_grad_hbm, n)),
        ]
        sent += start_copies(pairs, sems, len(copies) + 3 * n)
    wait_all(sent)


def prompt_far_kernel(
    core_ref, input_hbm, cot_hbm, logs_hbm, key_hbm, carried_hbm, pulled_hbm,
    near_input_hbm, near_key_hbm, near_query_hbm, own_hbm, got_hbm,
    input_grad_hbm, key_grad_hbm, query_grad_hbm,
    input_ref, cot_ref, logs_ref, key_ref, carried_ref, pulled_ref, near_input_ref, near_key_ref, near_query_ref,
    own_ref, got_ref, input_grad_ref, key_grad_ref, query_grad_ref, end_ref, start_ref, sems,
):
    chunks = carried_ref.shape[0]
    core = core_ref[0]
    order = range(chunks)
    pairs = [
        (own_hbm, own_ref), (got_hbm, got_ref), (logs_hbm, logs_ref), (key_hbm, key_ref), (input_hbm, input_ref),
        (cot_hbm, cot_ref), (near_key_hbm, near_key_ref), (near_query_hbm, near_query_ref),
    ]
    first = len(pairs)
    for three in zip(
        chunk_pairs(near_input_hbm, near_input_ref, order[::-1]), chunk_pairs(pulled_hbm, pulled_ref, order[::-1]),
        chunk_pairs(carried_hbm, carried_ref, order),
    ):
        pairs += three
    copies = start_copies(pairs, sems)
    wait_all(copies[:2])
    for place in range(own_ref.shape[0]):
        for ref, side_core in ((own_ref, core), (got_ref, 1 - core)):
            here = pl.ds(half_rows(place, side_core), PART)
            start_ref[here, :] = ref[place, :PART]
            end_ref[here, :] = ref[place, PART:]
    wait_all(copies[2:first])
    sent = []
    for step in range(chunks):
        wait_all(copies[first + 3 * step : first + 3 * step + 3])
        n = chunks - 1 - step
        here = slice(n * T, (n + 1) * T)
        sums, mid, last = chunk_logs(logs_ref, n)
        end = end_ref[...]
        end_ref[...] = rows(jnp.exp(last)) * end + pulled_ref[n]
        keys = tokens_of(key_ref, n)
        grow = rows(jnp.exp(mid - sums))
        in_high, in_low = split(lanes_of(input_ref, n).astype(F32) * grow)
        end_high, end_low = split(rows(jnp.exp(last - mid)) * end)
        input_grad = dot_nt(side(end_high, end_low), side(keys, keys))
        input_grad_ref[n] = (near_input_ref[n] + grow * input_grad).astype(BF16)
        pairs = [(input_grad_ref.at[n], lanes_at(input_grad_hbm, n))]
        sent += start_copies(pairs, sems, len(copies) + 3 * step)
        in_high_t, in_low_t = in_high.T, in_low.T
        both = dot(in_high_t, side(end_high, end_low))
        key_grad = both[:, :N] + (both[:, N:] + dot(in_low_t, end_high))
        key_grad_ref[here, :] = (near_key_ref[here, :] + key_grad).astype(BF16)
        pairs = [(tokens_at(key_grad_ref, n), tokens_at(key_grad_hbm, n))]
        sent += start_copies(pairs, sems, len(copies) + 3 * step + 1)

        n = step
        here = slice(n * T, (n + 1) * T)
        sums, mid, last = chunk_logs(logs_ref, n)
        start = start_ref[...]
        start_ref[...] = rows(jnp.exp(last)) * start + carried_ref[n]
        cot_high, cot_low = split(lanes_of(cot_ref, n).astype(F32) * rows(jnp.exp(sums - mid)))
        start_high, start_low = split(rows(jnp.exp(mid)) * start)
        cot_high_t, cot_low_t = cot_high.T, cot_low.T
        both = dot(cot_high_t, side(start_high, start_low))
        query_grad = both[:, :N] + (both[:, N:] + dot(cot_low_t, start_high))
        query_grad_ref[here, :] = (near_query_ref[here, :] + query_grad).astype(BF16)
        pairs = [(tokens_at(query_grad_ref, n), tokens_at(query_grad_hbm, n))]
        sent += start_copies(pairs, sems, len(copies) + 3 * step + 2)
    wait_all(sent)


def start_part_kernel(length_ref, core_ref, cot_ref, logs_ref, local_ref, state_ref, mine_ref, peer_ref):
    width = cot_ref.shape[0]
    state = jnp.concatenate([state_ref[place, STATES:] for place in range(state_ref.shape[0])], axis=0)
    state_high, state_low = split(state)
    total = jnp.zeros((logs_ref.shape[0], T), F32)
    for n in range(cot_ref.shape[1] // T):
        sums, _, last = chunk_logs(logs_ref, n)
        scaled = lanes_of(cot_ref, n).astype(F32) * rows(jnp.exp(total + sums))
        scaled = jnp.where(live_mask(n, length_ref[0], width), scaled, 0.0)
        high, low = split(scaled)
        high, low = high.T, low.T
        both = dot(high, side(state_high, state_low))
        part = both[:, :N] + (both[:, N:] + dot(low, state_high))
        by_core(n, core_ref[0], tokens_of(local_ref, n) + part, mine_ref, peer_ref)
        total = total + last


def tail_kernel(key_ref, query_mine_ref, query_got_ref, out_ref):
    out_ref[:, :PART] = key_ref[...]
    out_ref[:, PART:] = query_mine_ref[...] + query_got_ref[...]


def shape(*dims, dtype=F32):
    return jax.ShapeDtypeStruct(dims, dtype)


IN_HBM = pl.BlockSpec(memory_space=pltpu.HBM)
IN_VMEM = pl.BlockSpec(memory_space=pltpu.VMEM)


def held(*dims, dtype=F32):
    return pltpu.VMEM(dims, dtype)


def loading(kernel, scalars, far, outs):
    def run(*refs):
        first, sources, rest = refs[:scalars], refs[scalars : scalars + far], refs[scalars + far :]
        *rest, sems = rest
        targets, rest = rest[len(rest) - far :], rest[: len(rest) - far]
        wait_all(start_copies(list(zip(sources, targets)), sems))
        kernel(*first, *targets, *rest)

    return run


def call(kernel, outs, scratch=(), copies=0, scalars=0, far=0, count=0, far_outs=0, flops=0, name=None):
    def run(*args):
        sems, extra, inner = copies, [], kernel
        if far and not copies:
            sources = args[scalars : scalars + far]
            extra = [pltpu.VMEM(source.shape, source.dtype) for source in sources]
            sems, inner = far, loading(kernel, scalars, far, outs)
        return pl.pallas_call(
            inner,
            out_shape=outs,
            in_specs=[pl.BlockSpec(memory_space=pltpu.SMEM)] * scalars + [IN_HBM] * far + [IN_VMEM] * count,
            out_specs=[IN_HBM] * far_outs + [IN_VMEM] * (len(outs) - far_outs),
            scratch_shapes=list(scratch) + extra + ([pltpu.SemaphoreType.DMA((sems,))] if sems else []),
            compiler_params=pltpu.CompilerParams(vmem_limit_bytes=LARGE if sems else SMALL),
            cost_estimate=pl.CostEstimate(flops=flops, bytes_accessed=2000000, transcendentals=0),
            name=name,
        )(*args)

    return run


def body(
    prompt_inputs, prompt_keys, prompt_queries, prompt_logdecay, prompt_cotangent,
    answer_inputs, answer_keys, answer_queries, answer_logdecay, answer_cotangent, answer_lengths,
):
    tokens, heads, _ = prompt_inputs.shape
    _, length, answer_heads, _ = answer_inputs.shape
    width, answer_width = heads * HEAD, answer_heads * HEAD
    chunks, answer_chunks = tokens // T, length // T
    seq, comp = lax.axis_size("seq"), lax.axis_size("comp")
    quads = heads // answer_heads
    planes = seq // quads
    chips = seq // 2
    same_core = [[2 * chip + side for chip in range(chips)] for side in range(2)]
    same_pair = [[quads * plane + q for plane in range(planes)] for q in range(quads)]
    place = lax.axis_index("seq").astype(jnp.int32)
    group = (place // quads).reshape(1)
    core, y = place % 2, place // 2 % 2
    at = jnp.stack([core, y])
    core = core.reshape(1)

    def swap_cores(value):
        return lax.ppermute(value, "seq", [(i, i ^ 1) for i in range(seq)])

    def swap_chips(value):
        return lax.ppermute(value, "seq", [(i, i ^ 2) for i in range(seq)])

    def over(value, axis, groups=None):
        return lax.all_to_all(value, axis, 0, 0, axis_index_groups=groups, tiled=True)

    x = jnp.transpose(prompt_inputs, (1, 2, 0)).reshape(width, tokens)
    cot = jnp.transpose(prompt_cotangent, (1, 2, 0)).reshape(width, tokens)
    logs = prompt_logdecay.T
    keys, queries = prompt_keys.reshape(tokens, N), prompt_queries.reshape(tokens, N)
    ax = jnp.transpose(answer_inputs[0], (1, 2, 0)).reshape(answer_width, length)
    acot = jnp.transpose(answer_cotangent[0], (1, 2, 0)).reshape(answer_width, length)
    alogs = answer_logdecay[0].T
    all_keys, all_queries = answer_keys.reshape(length * GROUPS, N), answer_queries.reshape(length * GROUPS, N)

    prompt_lanes, prompt_rows = held(width, tokens, dtype=BF16), held(tokens, N, dtype=BF16)
    prompt_states = held(chunks, width, N)
    prompt_scratch = [prompt_lanes, prompt_lanes, held(heads, tokens), prompt_rows, prompt_rows]
    carried, pulled, mine, peer, totals = call(
        summary_kernel,
        [
            shape(chunks, width, N), shape(chunks, width, N), shape(chips, 2 * PART, N),
            shape(chips + 1, 2 * PART, N), shape(heads, N),
        ],
        scratch=prompt_scratch + [prompt_states, prompt_states, held(width, N), held(width, N)],
        copies=5 + 2 * chunks, scalars=1, far=5, far_outs=2, flops=10**9, name="prompt_summary",
    )(core, x, cot, logs, keys, queries)
    theirs = swap_cores(peer)

    answer_lanes, answer_rows = held(answer_width, length, dtype=BF16), held(length, N, dtype=BF16)
    answer_logs, answer_states = held(answer_heads, length), held(answer_chunks, answer_width, N)
    raw, raw_chunk = held(answer_chunks, T * GROUPS, N, dtype=BF16), held(2, T * GROUPS, N)
    ends, akeys, aqueries, start_grad = call(
        ends_kernel,
        [
            shape(answer_chunks, answer_width, N), shape(length, N, dtype=BF16), shape(length, N, dtype=BF16),
            shape(answer_width, N),
        ],
        scratch=[answer_lanes, answer_logs, answer_states, answer_rows, answer_rows, raw, raw, raw_chunk, raw_chunk],
        copies=4 + 3 * answer_chunks, scalars=2, far=4, far_outs=3, flops=10**9, name="answer_ends",
    )(answer_lengths, group, acot, alogs, all_keys, all_queries)
    half = shape(planes, 2 * PART, N)
    half_more = shape(planes + 1, 2 * PART, N)
    keep, away, chip_totals = call(
        pack_chip_kernel, [half, half_more, shape(heads, N)], scalars=1, count=3, flops=10**7, name="pack_chip"
    )(at, mine, theirs, totals)
    chip_theirs = swap_chips(away)
    (sent,) = call(
        pack_kernel, [shape(planes, GRADS + PART, N)], scalars=1, count=4, flops=10**7, name="pack"
    )(at, keep, chip_theirs, chip_totals, start_grad)
    blocks = over(sent, "seq", same_pair)

    near_input, near_key, near_query = call(
        prompt_near_kernel, [shape(chunks, width, T), shape(tokens, N), shape(tokens, N)],
        scratch=prompt_scratch + [held(chunks, width, T), held(tokens, N), held(tokens, N)],
        copies=5 + 3 * chunks, far=5, far_outs=3, flops=3 * 10**9, name="prompt_near",
    )(x, cot, logs, keys, queries)
    ax_grad, aq_local, key_mine, key_peer = call(
        answer_kernel,
        [
            shape(answer_width, length, dtype=BF16), shape(length, N),
            shape(chips, PART, N), shape(chips, PART, N),
        ],
        scratch=[
            answer_lanes, answer_lanes, answer_logs, answer_rows, answer_rows, answer_states,
            held(answer_chunks, answer_width, T, dtype=BF16), held(length, N), held(answer_width, N),
        ],
        copies=5 + 3 * answer_chunks, scalars=2, far=6, far_outs=2, flops=3 * 10**9, name="answer_grads",
    )(answer_lengths, core, ax, acot, alogs, akeys, aqueries, ends)

    starts, sent = call(
        scan_kernel, [shape(planes, PART, N), shape(comp, 2 * PART, N)], count=1, flops=10**7, name="scan"
    )(blocks)
    sent, ax_grad, aq_local, key_mine, key_peer = lax.optimization_barrier(
        (sent, ax_grad, aq_local, key_mine, key_peer)
    )
    finals = over(sent, "comp")
    key_parts = key_mine + swap_cores(key_peer)
    finals, near_input, near_key, near_query = lax.optimization_barrier((finals, near_input, near_key, near_query))
    (sent,) = call(
        scan_back_kernel, [shape(planes, 3 * PART, N)], count=3, flops=10**7, name="scan_back"
    )(blocks, starts, finals)
    states = over(sent, "seq", same_pair)
    chip_own, chip_other = call(
        unpack_kernel, [half, half], scalars=1, count=4, flops=10**7, name="unpack"
    )(at, keep, chip_theirs, chip_totals, states)
    chip_got = swap_chips(chip_other)

    query_mine, query_peer = call(
        start_part_kernel, [shape(chips, PART, N), shape(chips, PART, N)],
        scalars=2, far=3, count=1, flops=10**9, name="answer_start_part",
    )(answer_lengths, core, acot, alogs, aq_local, states)
    (sent,) = call(tail_kernel, [shape(chips, 2 * PART, N)], count=3, flops=10**7, name="pack_tail")(
        key_parts, query_mine, swap_cores(query_peer)
    )
    parts = over(sent, "seq", same_core)
    own, other = call(
        unpack_chip_kernel, [shape(chips, 2 * PART, N), shape(chips, 2 * PART, N)],
        scalars=1, count=5, flops=10**7, name="unpack_chip",
    )(at, mine, theirs, totals, chip_own, chip_got)
    x_grad, k_grad, q_grad = call(
        prompt_far_kernel,
        [shape(width, tokens, dtype=BF16), shape(tokens, N, dtype=BF16), shape(tokens, N, dtype=BF16)],
        scratch=[
            prompt_lanes, prompt_lanes, held(heads, tokens), prompt_rows, prompt_states, prompt_states,
            held(chunks, width, T), held(tokens, N), held(tokens, N),
            held(chips, 2 * PART, N), held(chips, 2 * PART, N),
            held(chunks, width, T, dtype=BF16), prompt_rows, prompt_rows, held(width, N), held(width, N),
        ],
        copies=8 + 6 * chunks, scalars=1, far=11, far_outs=3, flops=3 * 10**9, name="prompt_far",
    )(
        core, x, cot, logs, keys, carried, pulled, near_input, near_key, near_query, own, swap_cores(other),
    )

    gathered = shape(PART * GROUPS, N, dtype=BF16)
    key_out, query_out = call(
        gather_kernel, [gathered, gathered], scratch=[held(PART * GROUPS, N)],
        count=1, flops=10**7, name="gather_groups",
    )(parts)

    return (
        jnp.transpose(x_grad.reshape(heads, HEAD, tokens), (2, 0, 1)),
        k_grad.reshape(tokens, 1, N),
        q_grad.reshape(tokens, 1, N),
        jnp.transpose(ax_grad.reshape(answer_heads, HEAD, length), (2, 0, 1))[None],
        key_out.reshape(1, PART, GROUPS, N),
        query_out.reshape(1, PART, GROUPS, N),
    )


def solution(mesh):
    in_specs = (
        P("seq", "comp", None),
        P("seq", "comp", None),
        P("seq", "comp", None),
        P("seq", "comp"),
        P("seq", "comp", None),
        P("comp", None, "seq", None),
        P("comp", None, None, None),
        P("comp", None, None, None),
        P("comp", None, "seq"),
        P("comp", None, "seq", None),
        P("comp"),
    )
    out_specs = (
        P("seq", "comp", None),
        P("seq", "comp", None),
        P("seq", "comp", None),
        P("comp", None, "seq", None),
        P("comp", "seq", None, None),
        P("comp", "seq", None, None),
    )
    return jax.shard_map(body, mesh=mesh, in_specs=in_specs, out_specs=out_specs, check_vma=False)
```

```python
import functools

import jax
import jax.numpy as jnp
from jax import lax
from jax.experimental import pallas as pl
from jax.experimental.pallas import tpu as pltpu
from jax.sharding import PartitionSpec as P

F32 = jnp.float32
BF16 = jnp.bfloat16
T = 128
MID = 63
N = 128
GROUPS = 8
HEAD = 64
PART = 32
SMALL, LARGE = 16 * 1024 * 1024, 56 * 1024 * 1024


def dot(left, right):
    return lax.dot_general(left, right, (((1,), (0,)), ((), ())), preferred_element_type=F32)


def dot_nt(left, right):
    return lax.dot_general(left, right, (((1,), (1,)), ((), ())), preferred_element_type=F32)


def split(value):
    high = value.astype(BF16)
    return high, (value - high.astype(F32)).astype(BF16)


def running(logs):
    first, rest = split(logs)
    second, third = split(logs - first.astype(F32))
    upper = lax.broadcasted_iota(jnp.int32, (T, T), 0) <= lax.broadcasted_iota(jnp.int32, (T, T), 1)
    ones = jnp.where(upper, 1.0, 0.0).astype(BF16)
    return dot(first, ones) + (dot(second, ones) + dot(third, ones))


def rows(per_head):
    heads, lanes = per_head.shape
    spread = jnp.broadcast_to(per_head[:, None, :], (heads, HEAD, lanes))
    return spread.reshape(heads * HEAD, lanes)


def column(logs, token):
    return jnp.broadcast_to(logs[:, token : token + 1], logs.shape)


def chunk_logs(logs_ref, number):
    return block_logs(logs_ref[:, number * T : (number + 1) * T])


def block_logs(logs):
    sums = running(logs)
    return sums, column(sums, MID), column(sums, T - 1)


def tokens_of(ref, number):
    return ref[number * T : (number + 1) * T, :]


def lanes_at(ref, number):
    return ref.at[:, number * T : (number + 1) * T]


def tokens_at(ref, number, count=T):
    return ref.at[number * count : (number + 1) * count, :]


def start_copies(pairs, sems, first=0):
    copies = [pltpu.make_async_copy(source, target, sems.at[first + n]) for n, (source, target) in enumerate(pairs)]
    for copy in copies:
        copy.start()
    return copies


def wait_all(copies):
    for copy in copies:
        copy.wait()


def lanes_of(ref, number):
    return ref[:, number * T : (number + 1) * T]


def chunk_pairs(hbm_ref, ref, order):
    return [(hbm_ref.at[n], ref.at[n]) for n in order]


def live_mask(number, length, width):
    token = lax.broadcasted_iota(jnp.int32, (width, T), 1) + number * T
    return token < length


def twice(value):
    return jnp.concatenate([value, value], axis=0)


def side(left, right):
    return jnp.concatenate([left, right], axis=1)


def own_group(ref, group, all_ref):
    all_ref[...] = ref.astype(F32)
    return all_ref[pl.ds(group, T, stride=GROUPS), :].astype(BF16)


def ends_kernel(
    length_ref, group_ref, cot_hbm, logs_hbm, key_hbm, query_hbm, ends_hbm, own_key_hbm, own_query_hbm, start_ref,
    cot_ref, logs_ref, ends_ref, own_key_ref, own_query_ref, raw_k, raw_q, all_k, all_q, sems,
):
    chunks, width = ends_ref.shape[0], ends_ref.shape[1]
    order = list(range(chunks - 1, -1, -1))
    raw_pairs = [(tokens_at(query_hbm, n, T * GROUPS), raw_q.at[n]) for n in order]
    pairs = [(logs_hbm, logs_ref), (cot_hbm, cot_ref)] + raw_pairs
    pairs += [(tokens_at(key_hbm, n, T * GROUPS), raw_k.at[n]) for n in order]
    copies = start_copies(pairs, sems)
    wait_all(copies[:2])
    current = jnp.zeros((width, N), F32)
    sent = []
    for step, n in enumerate(order):
        copies[2 + step].wait()
        queries = own_group(raw_q[n], group_ref[0], all_q.at[step % 2])
        own_query_ref[n * T : (n + 1) * T, :] = queries
        sums, mid, last = chunk_logs(logs_ref, n)
        scaled = lanes_of(cot_ref, n).astype(F32) * rows(jnp.exp(sums - mid))
        scaled = jnp.where(live_mask(n, length_ref[0], width), scaled, 0.0)
        high, low = split(scaled)
        pulled = dot(side(high, low), twice(queries))
        ends_ref[n] = current
        sent += start_copies([(ends_ref.at[n], ends_hbm.at[n])], sems, len(copies) + step)
        current = rows(jnp.exp(last)) * current + rows(jnp.exp(mid)) * pulled
    start_ref[...] = current
    for step, n in enumerate(order):
        copies[2 + chunks + step].wait()
        own_key_ref[n * T : (n + 1) * T, :] = own_group(raw_k[n], group_ref[0], all_k.at[step % 2])
    pairs = [(own_key_ref, own_key_hbm), (own_query_ref, own_query_hbm)]
    wait_all(sent + start_copies(pairs, sems, len(copies) + chunks))


PLANES = 8


def half_rows(place, core):
    return pl.multiple_of((place // PLANES) * 8 * HEAD + core * 4 * HEAD + (place % PLANES) * PART, PART)


def summary_kernel(
    core_ref, input_hbm, cot_hbm, logs_hbm, key_hbm, query_hbm,
    carried_hbm, pulled_hbm, mine_ref, peer_ref, total_ref,
    input_ref, cot_ref, logs_ref, key_ref, query_ref, carried_ref, pulled_ref, all_c, all_p, sems,
):
    chunks = carried_ref.shape[0]
    order = range(chunks)
    pairs = [
        (logs_hbm, logs_ref), (key_hbm, key_ref), (input_hbm, input_ref), (query_hbm, query_ref), (cot_hbm, cot_ref)
    ]
    copies = start_copies(pairs, sems)
    wait_all(copies[:3])
    total = jnp.zeros(total_ref.shape, F32)
    sent = []
    for n in order:
        sums, mid, last = chunk_logs(logs_ref, n)
        high, low = split(lanes_of(input_ref, n).astype(F32) * rows(jnp.exp(mid - sums)))
        carried = dot(side(high, low), twice(tokens_of(key_ref, n)))
        carried = rows(jnp.exp(last - mid)) * carried
        carried_ref[n] = carried
        sent += start_copies([(carried_ref.at[n], carried_hbm.at[n])], sems, len(copies) + 2 * n)
        all_c[...] = carried if n == 0 else rows(jnp.exp(last)) * all_c[...] + carried
        if n == 0:
            wait_all(copies[3:])
        high, low = split(lanes_of(cot_ref, n).astype(F32) * rows(jnp.exp(sums - mid)))
        pulled = dot(side(high, low), twice(tokens_of(query_ref, n)))
        pulled = rows(jnp.exp(mid)) * pulled
        pulled_ref[n] = pulled
        sent += start_copies([(pulled_ref.at[n], pulled_hbm.at[n])], sems, len(copies) + 2 * n + 1)
        all_p[...] = pulled if n == 0 else all_p[...] + rows(jnp.exp(total)) * pulled
        total = total + last
    total_ref[...] = total
    core = core_ref[0]
    places = mine_ref.shape[0]
    for place in range(places):
        for ref, side_core in ((mine_ref, core), (peer_ref, 1 - core)):
            here = pl.ds(half_rows(place, side_core), PART)
            ref[place, :PART] = all_c[here, :]
            ref[place, PART:] = all_p[here, :]
    heads = total_ref.shape[0]
    peer_ref[places, :heads] = total_ref[...]
    peer_ref[places, heads:] = jnp.zeros_like(peer_ref[places, heads:])
    wait_all(sent)


def both_totals(first, head, mine_ref, got_ref):
    mine = mine_ref[pl.ds(head, 1), :]
    theirs = got_ref[got_ref.shape[0] - 1, pl.ds(head, 1), :]
    return jnp.where(first, mine, theirs), jnp.where(first, theirs, mine)


STATES = 2 * PART
GRADS = STATES + 8
KEYS = STATES + PART


def head_of(place, side_y, core):
    return side_y * 8 + core * 4 + place * PART // HEAD


def joined(first, mine, theirs, total0, total1):
    zero, one = jnp.where(first, mine, theirs), jnp.where(first, theirs, mine)
    return jnp.exp(total1) * zero[:PART] + one[:PART], zero[PART:] + jnp.exp(total0) * one[PART:]


def parted(first, mine, theirs, total0, total1, start, end):
    carried0 = jnp.where(first, mine[:PART], theirs[:PART])
    pulled1 = jnp.where(first, theirs[PART:], mine[PART:])
    start1 = jnp.exp(total0) * start + carried0
    end0 = jnp.exp(total1) * end + pulled1
    own = jnp.where(first, start, start1), jnp.where(first, end0, end)
    return own, (jnp.where(first, start1, start), jnp.where(first, end, end0))


def pack_chip_kernel(at_ref, mine_ref, got_ref, total_ref, keep_ref, away_ref, chip_total_ref):
    core, y = at_ref[0], at_ref[1]
    heads = total_ref.shape[0]
    chip_total_ref[...] = total_ref[...] + got_ref[got_ref.shape[0] - 1, :heads]
    for place in range(PLANES):
        for ref, side_y in ((keep_ref, y), (away_ref, 1 - y)):
            total0, total1 = both_totals(core == 0, head_of(place, side_y, core), total_ref, got_ref)
            here = side_y * PLANES + place
            carried, pulled = joined(core == 0, mine_ref[here], got_ref[here], total0, total1)
            ref[place, :PART] = carried
            ref[place, PART:] = pulled
    away_ref[PLANES, :heads] = chip_total_ref[...]
    away_ref[PLANES, heads:] = jnp.zeros_like(away_ref[PLANES, heads:])


def pack_kernel(at_ref, keep_ref, got_ref, total_ref, start_ref, out_ref):
    core, y = at_ref[0], at_ref[1]
    for place in range(PLANES):
        total0, total1 = both_totals(y == 0, head_of(place, y, core), total_ref, got_ref)
        carried, pulled = joined(y == 0, keep_ref[place], got_ref[place], total0, total1)
        out_ref[place, :PART] = carried
        out_ref[place, PART:STATES] = pulled
        out_ref[place, STATES:GRADS] = jnp.broadcast_to(total0 + total1, (8, N))
        out_ref[place, GRADS:] = start_ref[PART * place : PART * (place + 1)]


def scan_kernel(blocks_ref, starts_ref, out_ref):
    current = jnp.zeros((PART, N), F32)
    for place in range(PLANES):
        starts_ref[place] = current
        current = jnp.exp(blocks_ref[place, STATES : STATES + 1]) * current + blocks_ref[place, :PART]
    for group in range(out_ref.shape[0]):
        out_ref[group, :PART] = blocks_ref[group, GRADS:]
        out_ref[group, PART:] = current


def key_chip_kernel(at_ref, mine_ref, got_ref, keep_ref, away_ref):
    y = at_ref[1]
    keep_ref[...] = mine_ref[pl.ds(y * PLANES, PLANES)] + got_ref[pl.ds(y * PLANES, PLANES)]
    away_ref[...] = mine_ref[pl.ds((1 - y) * PLANES, PLANES)] + got_ref[pl.ds((1 - y) * PLANES, PLANES)]


def scan_back_kernel(blocks_ref, starts_ref, got_ref, key_keep_ref, key_got_ref, out_ref):
    current = got_ref[0, :PART]
    for answer in range(1, got_ref.shape[0]):
        current = current + got_ref[answer, :PART]
    for place in range(PLANES - 1, -1, -1):
        out_ref[place, :PART] = starts_ref[place]
        out_ref[place, PART:STATES] = current
        out_ref[place, STATES:KEYS] = got_ref[place, PART:]
        out_ref[place, KEYS:] = key_keep_ref[place] + key_got_ref[place]
        current = jnp.exp(blocks_ref[place, STATES : STATES + 1]) * current + blocks_ref[place, PART:STATES]


def unpack_kernel(at_ref, keep_ref, got_ref, total_ref, states_ref, own_ref, other_ref, key_ref, sums_ref):
    for group in range(GROUPS):
        sums_ref[pl.ds(group, PART, stride=GROUPS), :] = states_ref[group, KEYS:]
    key_ref[...] = sums_ref[...].astype(BF16)
    core, y = at_ref[0], at_ref[1]
    for place in range(PLANES):
        total0, total1 = both_totals(y == 0, head_of(place, y, core), total_ref, got_ref)
        own, other = parted(
            y == 0, keep_ref[place], got_ref[place], total0, total1,
            states_ref[place, :PART], states_ref[place, PART:STATES],
        )
        for ref, (start, end) in ((own_ref, own), (other_ref, other)):
            ref[place, :PART] = start
            ref[place, PART:] = end


def unpack_chip_kernel(at_ref, mine_ref, got_ref, total_ref, near_ref, away_ref, own_ref, other_ref):
    core, y = at_ref[0], at_ref[1]
    for place in range(PLANES):
        for chip_ref, side_y in ((near_ref, y), (away_ref, 1 - y)):
            total0, total1 = both_totals(core == 0, head_of(place, side_y, core), total_ref, got_ref)
            here = side_y * PLANES + place
            own, other = parted(
                core == 0, mine_ref[here], got_ref[here], total0, total1,
                chip_ref[place, :PART], chip_ref[place, PART:],
            )
            for ref, (start, end) in ((own_ref, own), (other_ref, other)):
                ref[here, :PART] = start
                ref[here, PART:] = end


def gather_kernel(parts_ref, query_ref, sums_ref):
    for group in range(GROUPS):
        sums_ref[pl.ds(group, PART, stride=GROUPS), :] = parts_ref[2 * group] + parts_ref[2 * group + 1]
    query_ref[...] = sums_ref[...].astype(BF16)


def chunk_grads(inputs, cot, logs3, keys, queries, start, end):
    sums, mid, last = logs3
    grow = rows(jnp.exp(mid - sums))
    fall = rows(jnp.exp(sums - mid))
    in_high, in_low = split(inputs * grow)
    cot_high, cot_low = split(cot * fall)
    end_high, end_low = split(rows(jnp.exp(last - mid)) * end)
    start_high, start_low = split(rows(jnp.exp(mid)) * start)
    first = lax.broadcasted_iota(jnp.int32, (T, T), 0)
    second = lax.broadcasted_iota(jnp.int32, (T, T), 1)
    score_high, score_low = split(jnp.where(first >= second, dot_nt(queries, keys), 0.0))
    input_grad = dot(side(cot_high, cot_low), twice(score_high)) + dot(cot_high, score_low)
    input_grad = input_grad + dot_nt(side(end_high, end_low), side(keys, keys))
    input_grad = grow * input_grad
    in_high_t, in_low_t = in_high.T, in_low.T
    right_high, right_low = side(cot_high, end_high), side(cot_low, end_low)
    both = dot(in_high_t, right_high) + (dot(in_high_t, right_low) + dot(in_low_t, right_high))
    products = jnp.where(second >= first, both[:, :T], 0.0)
    high, low = split(products)
    key_grad = both[:, T:] + dot(side(high, low), twice(queries))
    high, low = split(products.T)
    query_grad = dot(side(high, low), twice(keys))
    cot_high_t, cot_low_t = cot_high.T, cot_low.T
    query_grad = query_grad + dot(cot_high_t, start_high)
    query_grad = query_grad + (dot(cot_high_t, start_low) + dot(cot_low_t, start_high))
    return input_grad, key_grad, query_grad, (in_high, in_low)


def by_core(number, core, value, mine_ref, peer_ref):
    value = value.reshape(2, 2, PART, N)
    here = pl.ds(2 * number, 2)
    mine_ref[here] = jnp.where(core == 0, value[:, 0], value[:, 1])
    peer_ref[here] = jnp.where(core == 0, value[:, 1], value[:, 0])


def answer_kernel(
    length_ref, core_ref, input_hbm, cot_hbm, logs_hbm, key_hbm, query_hbm, ends_hbm,
    input_grad_hbm, query_grad_hbm, key_mine_ref, key_peer_ref,
    input_ref, cot_ref, logs_ref, key_ref, query_ref, ends_ref, input_grad_ref, query_grad_ref, state_ref, sems,
):
    chunks, width = ends_ref.shape[0], ends_ref.shape[1]
    order = range(chunks)
    pairs = [
        (logs_hbm, logs_ref), (key_hbm, key_ref), (query_hbm, query_ref), (input_hbm, input_ref), (cot_hbm, cot_ref)
    ]
    copies = start_copies(pairs + chunk_pairs(ends_hbm, ends_ref, order), sems)
    wait_all(copies[:5])
    state_ref[...] = jnp.zeros_like(state_ref)
    sent = []
    for n in order:
        logs3 = chunk_logs(logs_ref, n)
        sums, mid, last = logs3
        copies[5 + n].wait()
        cot = jnp.where(live_mask(n, length_ref[0], width), lanes_of(cot_ref, n).astype(F32), 0.0)
        keys, queries = tokens_of(key_ref, n), tokens_of(query_ref, n)
        start = state_ref[...]
        input_grad, key_grad, query_grad, (high, low) = chunk_grads(
            lanes_of(input_ref, n).astype(F32), cot, logs3, keys, queries, start, ends_ref[n]
        )
        input_grad_ref[n] = input_grad.astype(BF16)
        for side_y in range(2):
            first, second = (key_grad[PART * row : PART * (row + 1)] for row in (2 * side_y, 2 * side_y + 1))
            key_mine_ref[side_y * PLANES + n] = jnp.where(core_ref[0] == 0, first, second)
            key_peer_ref[side_y * PLANES + n] = jnp.where(core_ref[0] == 0, second, first)
        query_grad_ref[n * T : (n + 1) * T, :] = query_grad
        pairs = [
            (input_grad_ref.at[n], lanes_at(input_grad_hbm, n)),
            (tokens_at(query_grad_ref, n), tokens_at(query_grad_hbm, n)),
        ]
        sent += start_copies(pairs, sems, len(copies) + 2 * n)
        carried = dot(side(high, low), twice(keys))
        state_ref[...] = rows(jnp.exp(last)) * start + rows(jnp.exp(last - mid)) * carried
    wait_all(sent)


def prompt_near_kernel(
    input_hbm, cot_hbm, logs_hbm, key_hbm, query_hbm, input_grad_hbm, key_grad_hbm, query_grad_hbm,
    input_ref, cot_ref, logs_ref, key_ref, query_ref, input_grad_ref, key_grad_ref, query_grad_ref, sems,
):
    first = lax.broadcasted_iota(jnp.int32, (T, T), 0)
    second = lax.broadcasted_iota(jnp.int32, (T, T), 1)
    order = range(input_ref.shape[1] // T)
    pairs = [
        (logs_hbm, logs_ref), (key_hbm, key_ref), (query_hbm, query_ref), (input_hbm, input_ref), (cot_hbm, cot_ref)
    ]
    copies = start_copies(pairs, sems)
    wait_all(copies)
    sent = []
    for n in order:
        here = slice(n * T, (n + 1) * T)
        sums, mid, _ = chunk_logs(logs_ref, n)
        keys, queries = tokens_of(key_ref, n), tokens_of(query_ref, n)
        grow = rows(jnp.exp(mid - sums))
        in_high, in_low = split(lanes_of(input_ref, n).astype(F32) * grow)
        cot_high, cot_low = split(lanes_of(cot_ref, n).astype(F32) * rows(jnp.exp(sums - mid)))
        score_high, score_low = split(jnp.where(first >= second, dot_nt(queries, keys), 0.0))
        input_grad = dot(side(cot_high, cot_low), twice(score_high)) + dot(cot_high, score_low)
        input_grad_ref[n] = grow * input_grad
        in_high_t, in_low_t = in_high.T, in_low.T
        both = dot(in_high_t, side(cot_high, cot_low))
        products = both[:, :T] + (both[:, T:] + dot(in_low_t, cot_high))
        products = jnp.where(second >= first, products, 0.0)
        high, low = split(products)
        key_grad_ref[here, :] = dot(side(high, low), twice(queries))
        high, low = split(products.T)
        query_grad_ref[here, :] = dot(side(high, low), twice(keys))
        pairs = [
            (input_grad_ref.at[n], input_grad_hbm.at[n]),
            (tokens_at(key_grad_ref, n), tokens_at(key_grad_hbm, n)),
            (tokens_at(query_grad_ref, n), tokens_at(query_grad_hbm, n)),
        ]
        sent += start_copies(pairs, sems, len(copies) + 3 * n)
    wait_all(sent)


def prompt_far_kernel(
    core_ref, input_hbm, cot_hbm, logs_hbm, key_hbm, carried_hbm, pulled_hbm,
    near_input_hbm, near_key_hbm, near_query_hbm, own_hbm, got_hbm,
    input_grad_hbm, key_grad_hbm, query_grad_hbm,
    input_ref, cot_ref, logs_ref, key_ref, carried_ref, pulled_ref, near_input_ref, near_key_ref, near_query_ref,
    own_ref, got_ref, input_grad_ref, key_grad_ref, query_grad_ref, end_ref, start_ref, sems,
):
    chunks = carried_ref.shape[0]
    core = core_ref[0]
    order = range(chunks)
    pairs = [
        (own_hbm, own_ref), (got_hbm, got_ref), (logs_hbm, logs_ref), (key_hbm, key_ref), (input_hbm, input_ref),
        (cot_hbm, cot_ref), (near_key_hbm, near_key_ref), (near_query_hbm, near_query_ref),
    ]
    first = len(pairs)
    for three in zip(
        chunk_pairs(near_input_hbm, near_input_ref, order[::-1]), chunk_pairs(pulled_hbm, pulled_ref, order[::-1]),
        chunk_pairs(carried_hbm, carried_ref, order),
    ):
        pairs += three
    copies = start_copies(pairs, sems)
    wait_all(copies[:2])
    for place in range(own_ref.shape[0]):
        for ref, side_core in ((own_ref, core), (got_ref, 1 - core)):
            here = pl.ds(half_rows(place, side_core), PART)
            start_ref[here, :] = ref[place, :PART]
            end_ref[here, :] = ref[place, PART:]
    wait_all(copies[2:first])
    sent = []
    for step in range(chunks):
        wait_all(copies[first + 3 * step : first + 3 * step + 3])
        n = chunks - 1 - step
        here = slice(n * T, (n + 1) * T)
        sums, mid, last = chunk_logs(logs_ref, n)
        end = end_ref[...]
        end_ref[...] = rows(jnp.exp(last)) * end + pulled_ref[n]
        keys = tokens_of(key_ref, n)
        grow = rows(jnp.exp(mid - sums))
        in_high, in_low = split(lanes_of(input_ref, n).astype(F32) * grow)
        end_high, end_low = split(rows(jnp.exp(last - mid)) * end)
        input_grad = dot_nt(side(end_high, end_low), side(keys, keys))
        input_grad_ref[n] = (near_input_ref[n] + grow * input_grad).astype(BF16)
        pairs = [(input_grad_ref.at[n], lanes_at(input_grad_hbm, n))]
        sent += start_copies(pairs, sems, len(copies) + 3 * step)
        in_high_t, in_low_t = in_high.T, in_low.T
        both = dot(in_high_t, side(end_high, end_low))
        key_grad = both[:, :N] + (both[:, N:] + dot(in_low_t, end_high))
        key_grad_ref[here, :] = (near_key_ref[here, :] + key_grad).astype(BF16)
        pairs = [(tokens_at(key_grad_ref, n), tokens_at(key_grad_hbm, n))]
        sent += start_copies(pairs, sems, len(copies) + 3 * step + 1)

        n = step
        here = slice(n * T, (n + 1) * T)
        sums, mid, last = chunk_logs(logs_ref, n)
        start = start_ref[...]
        start_ref[...] = rows(jnp.exp(last)) * start + carried_ref[n]
        cot_high, cot_low = split(lanes_of(cot_ref, n).astype(F32) * rows(jnp.exp(sums - mid)))
        start_high, start_low = split(rows(jnp.exp(mid)) * start)
        cot_high_t, cot_low_t = cot_high.T, cot_low.T
        both = dot(cot_high_t, side(start_high, start_low))
        query_grad = both[:, :N] + (both[:, N:] + dot(cot_low_t, start_high))
        query_grad_ref[here, :] = (near_query_ref[here, :] + query_grad).astype(BF16)
        pairs = [(tokens_at(query_grad_ref, n), tokens_at(query_grad_hbm, n))]
        sent += start_copies(pairs, sems, len(copies) + 3 * step + 2)
    wait_all(sent)


def start_part_kernel(length_ref, core_ref, cot_ref, logs_ref, local_ref, state_ref, mine_ref, peer_ref):
    width = cot_ref.shape[0]
    state = jnp.concatenate([state_ref[place, STATES:KEYS] for place in range(state_ref.shape[0])], axis=0)
    state_high, state_low = split(state)
    total = jnp.zeros((logs_ref.shape[0], T), F32)
    for n in range(cot_ref.shape[1] // T):
        sums, _, last = chunk_logs(logs_ref, n)
        scaled = lanes_of(cot_ref, n).astype(F32) * rows(jnp.exp(total + sums))
        scaled = jnp.where(live_mask(n, length_ref[0], width), scaled, 0.0)
        high, low = split(scaled)
        high, low = high.T, low.T
        both = dot(high, side(state_high, state_low))
        part = both[:, :N] + (both[:, N:] + dot(low, state_high))
        by_core(n, core_ref[0], tokens_of(local_ref, n) + part, mine_ref, peer_ref)
        total = total + last


def shape(*dims, dtype=F32):
    return jax.ShapeDtypeStruct(dims, dtype)


IN_HBM = pl.BlockSpec(memory_space=pltpu.HBM)
IN_VMEM = pl.BlockSpec(memory_space=pltpu.VMEM)


def held(*dims, dtype=F32):
    return pltpu.VMEM(dims, dtype)


def loading(kernel, scalars, far, outs):
    def run(*refs):
        first, sources, rest = refs[:scalars], refs[scalars : scalars + far], refs[scalars + far :]
        *rest, sems = rest
        targets, rest = rest[len(rest) - far :], rest[: len(rest) - far]
        wait_all(start_copies(list(zip(sources, targets)), sems))
        kernel(*first, *targets, *rest)

    return run


def call(kernel, outs, scratch=(), copies=0, scalars=0, far=0, count=0, far_outs=0, flops=0, name=None):
    def run(*args):
        sems, extra, inner = copies, [], kernel
        if far and not copies:
            sources = args[scalars : scalars + far]
            extra = [pltpu.VMEM(source.shape, source.dtype) for source in sources]
            sems, inner = far, loading(kernel, scalars, far, outs)
        return pl.pallas_call(
            inner,
            out_shape=outs,
            in_specs=[pl.BlockSpec(memory_space=pltpu.SMEM)] * scalars + [IN_HBM] * far + [IN_VMEM] * count,
            out_specs=[IN_HBM] * far_outs + [IN_VMEM] * (len(outs) - far_outs),
            scratch_shapes=list(scratch) + extra + ([pltpu.SemaphoreType.DMA((sems,))] if sems else []),
            compiler_params=pltpu.CompilerParams(vmem_limit_bytes=LARGE if sems else SMALL),
            cost_estimate=pl.CostEstimate(flops=flops, bytes_accessed=2000000, transcendentals=0),
            name=name,
        )(*args)

    return run


def body(
    prompt_inputs, prompt_keys, prompt_queries, prompt_logdecay, prompt_cotangent,
    answer_inputs, answer_keys, answer_queries, answer_logdecay, answer_cotangent, answer_lengths,
):
    tokens, heads, _ = prompt_inputs.shape
    _, length, answer_heads, _ = answer_inputs.shape
    width, answer_width = heads * HEAD, answer_heads * HEAD
    chunks, answer_chunks = tokens // T, length // T
    seq, comp = lax.axis_size("seq"), lax.axis_size("comp")
    quads = heads // answer_heads
    planes = seq // quads
    chips = seq // 2
    same_core = [[2 * chip + side for chip in range(chips)] for side in range(2)]
    same_pair = [[quads * plane + q for plane in range(planes)] for q in range(quads)]
    place = lax.axis_index("seq").astype(jnp.int32)
    group = (place // quads).reshape(1)
    core, y = place % 2, place // 2 % 2
    at = jnp.stack([core, y])
    core = core.reshape(1)

    def swap_cores(value):
        return lax.ppermute(value, "seq", [(i, i ^ 1) for i in range(seq)])

    def swap_chips(value):
        return lax.ppermute(value, "seq", [(i, i ^ 2) for i in range(seq)])

    def over(value, axis, groups=None):
        return lax.all_to_all(value, axis, 0, 0, axis_index_groups=groups, tiled=True)

    x = jnp.transpose(prompt_inputs, (1, 2, 0)).reshape(width, tokens)
    cot = jnp.transpose(prompt_cotangent, (1, 2, 0)).reshape(width, tokens)
    logs = prompt_logdecay.T
    keys, queries = prompt_keys.reshape(tokens, N), prompt_queries.reshape(tokens, N)
    ax = jnp.transpose(answer_inputs[0], (1, 2, 0)).reshape(answer_width, length)
    acot = jnp.transpose(answer_cotangent[0], (1, 2, 0)).reshape(answer_width, length)
    alogs = answer_logdecay[0].T
    all_keys, all_queries = answer_keys.reshape(length * GROUPS, N), answer_queries.reshape(length * GROUPS, N)

    prompt_lanes, prompt_rows = held(width, tokens, dtype=BF16), held(tokens, N, dtype=BF16)
    prompt_states = held(chunks, width, N)
    prompt_scratch = [prompt_lanes, prompt_lanes, held(heads, tokens), prompt_rows, prompt_rows]
    carried, pulled, mine, peer, totals = call(
        summary_kernel,
        [
            shape(chunks, width, N), shape(chunks, width, N), shape(chips, 2 * PART, N),
            shape(chips + 1, 2 * PART, N), shape(heads, N),
        ],
        scratch=prompt_scratch + [prompt_states, prompt_states, held(width, N), held(width, N)],
        copies=5 + 2 * chunks, scalars=1, far=5, far_outs=2, flops=10**9, name="prompt_summary",
    )(core, x, cot, logs, keys, queries)
    theirs = swap_cores(peer)

    answer_lanes, answer_rows = held(answer_width, length, dtype=BF16), held(length, N, dtype=BF16)
    answer_logs, answer_states = held(answer_heads, length), held(answer_chunks, answer_width, N)
    raw, raw_chunk = held(answer_chunks, T * GROUPS, N, dtype=BF16), held(2, T * GROUPS, N)
    ends, akeys, aqueries, start_grad = call(
        ends_kernel,
        [
            shape(answer_chunks, answer_width, N), shape(length, N, dtype=BF16), shape(length, N, dtype=BF16),
            shape(answer_width, N),
        ],
        scratch=[answer_lanes, answer_logs, answer_states, answer_rows, answer_rows, raw, raw, raw_chunk, raw_chunk],
        copies=4 + 3 * answer_chunks, scalars=2, far=4, far_outs=3, flops=10**9, name="answer_ends",
    )(answer_lengths, group, acot, alogs, all_keys, all_queries)
    half = shape(planes, 2 * PART, N)
    half_more = shape(planes + 1, 2 * PART, N)
    keep, away, chip_totals = call(
        pack_chip_kernel, [half, half_more, shape(heads, N)], scalars=1, count=3, flops=10**7, name="pack_chip"
    )(at, mine, theirs, totals)
    chip_theirs = swap_chips(away)
    (sent,) = call(
        pack_kernel, [shape(planes, GRADS + PART, N)], scalars=1, count=4, flops=10**7, name="pack"
    )(at, keep, chip_theirs, chip_totals, start_grad)
    blocks = over(sent, "seq", same_pair)

    near_input, near_key, near_query = call(
        prompt_near_kernel, [shape(chunks, width, T), shape(tokens, N), shape(tokens, N)],
        scratch=prompt_scratch + [held(chunks, width, T), held(tokens, N), held(tokens, N)],
        copies=5 + 3 * chunks, far=5, far_outs=3, flops=3 * 10**9, name="prompt_near",
    )(x, cot, logs, keys, queries)
    ax_grad, aq_local, key_mine, key_peer = call(
        answer_kernel,
        [
            shape(answer_width, length, dtype=BF16), shape(length, N),
            shape(chips, PART, N), shape(chips, PART, N),
        ],
        scratch=[
            answer_lanes, answer_lanes, answer_logs, answer_rows, answer_rows, answer_states,
            held(answer_chunks, answer_width, T, dtype=BF16), held(length, N), held(answer_width, N),
        ],
        copies=5 + 3 * answer_chunks, scalars=2, far=6, far_outs=2, flops=3 * 10**9, name="answer_grads",
    )(answer_lengths, core, ax, acot, alogs, akeys, aqueries, ends)

    starts, sent = call(
        scan_kernel, [shape(planes, PART, N), shape(comp, 2 * PART, N)], count=1, flops=10**7, name="scan"
    )(blocks)
    sent, ax_grad, aq_local, key_mine, key_peer = lax.optimization_barrier(
        (sent, ax_grad, aq_local, key_mine, key_peer)
    )
    finals = over(sent, "comp")
    key_part = shape(planes, PART, N)
    key_keep, key_away = call(key_chip_kernel, [key_part, key_part], scalars=1, count=2, flops=10**7, name="key_chip")(
        at, key_mine, swap_cores(key_peer)
    )
    key_got = swap_chips(key_away)
    finals, near_input, near_key, near_query = lax.optimization_barrier((finals, near_input, near_key, near_query))
    (sent,) = call(
        scan_back_kernel, [shape(planes, KEYS + PART, N)], count=5, flops=10**7, name="scan_back"
    )(blocks, starts, finals, key_keep, key_got)
    states = over(sent, "seq", same_pair)
    gathered = shape(PART * GROUPS, N, dtype=BF16)
    chip_own, chip_other, key_out = call(
        unpack_kernel, [half, half, gathered], scratch=[held(PART * GROUPS, N)],
        scalars=1, count=4, flops=10**7, name="unpack",
    )(at, keep, chip_theirs, chip_totals, states)
    states, chip_own, chip_other = lax.optimization_barrier((states, chip_own, chip_other))
    chip_got = swap_chips(chip_other)

    query_mine, query_peer = call(
        start_part_kernel, [shape(chips, PART, N), shape(chips, PART, N)],
        scalars=2, far=3, count=1, flops=10**9, name="answer_start_part",
    )(answer_lengths, core, acot, alogs, aq_local, states)
    own, other = call(
        unpack_chip_kernel, [shape(chips, 2 * PART, N), shape(chips, 2 * PART, N)],
        scalars=1, count=5, flops=10**7, name="unpack_chip",
    )(at, mine, theirs, totals, chip_own, chip_got)
    sent, own, other = lax.optimization_barrier((query_mine + swap_cores(query_peer), own, other))
    parts = over(sent, "seq", same_core)
    x_grad, k_grad, q_grad = call(
        prompt_far_kernel,
        [shape(width, tokens, dtype=BF16), shape(tokens, N, dtype=BF16), shape(tokens, N, dtype=BF16)],
        scratch=[
            prompt_lanes, prompt_lanes, held(heads, tokens), prompt_rows, prompt_states, prompt_states,
            held(chunks, width, T), held(tokens, N), held(tokens, N),
            held(chips, 2 * PART, N), held(chips, 2 * PART, N),
            held(chunks, width, T, dtype=BF16), prompt_rows, prompt_rows, held(width, N), held(width, N),
        ],
        copies=8 + 6 * chunks, scalars=1, far=11, far_outs=3, flops=3 * 10**9, name="prompt_far",
    )(
        core, x, cot, logs, keys, carried, pulled, near_input, near_key, near_query, own, swap_cores(other),
    )

    (query_out,) = call(
        gather_kernel, [gathered], scratch=[held(PART * GROUPS, N)], count=1, flops=10**7, name="gather_groups"
    )(parts)

    return (
        jnp.transpose(x_grad.reshape(heads, HEAD, tokens), (2, 0, 1)),
        k_grad.reshape(tokens, 1, N),
        q_grad.reshape(tokens, 1, N),
        jnp.transpose(ax_grad.reshape(answer_heads, HEAD, length), (2, 0, 1))[None],
        key_out.reshape(1, PART, GROUPS, N),
        query_out.reshape(1, PART, GROUPS, N),
    )


def solution(mesh):
    in_specs = (
        P("seq", "comp", None),
        P("seq", "comp", None),
        P("seq", "comp", None),
        P("seq", "comp"),
        P("seq", "comp", None),
        P("comp", None, "seq", None),
        P("comp", None, None, None),
        P("comp", None, None, None),
        P("comp", None, "seq"),
        P("comp", None, "seq", None),
        P("comp"),
    )
    out_specs = (
        P("seq", "comp", None),
        P("seq", "comp", None),
        P("seq", "comp", None),
        P("comp", None, "seq", None),
        P("comp", "seq", None, None),
        P("comp", "seq", None, None),
    )
    return jax.shard_map(body, mesh=mesh, in_specs=in_specs, out_specs=out_specs, check_vma=False)
```

```python
import functools

import jax
import jax.numpy as jnp
from jax import lax
from jax.experimental import pallas as pl
from jax.experimental.pallas import tpu as pltpu
from jax.sharding import PartitionSpec as P

F32 = jnp.float32
BF16 = jnp.bfloat16
T = 128
MID = 63
N = 128
GROUPS = 8
HEAD = 64
PART = 32
SMALL, LARGE = 16 * 1024 * 1024, 56 * 1024 * 1024


def dot(left, right):
    return lax.dot_general(left, right, (((1,), (0,)), ((), ())), preferred_element_type=F32)


def dot_nt(left, right):
    return lax.dot_general(left, right, (((1,), (1,)), ((), ())), preferred_element_type=F32)


def split(value):
    high = value.astype(BF16)
    return high, (value - high.astype(F32)).astype(BF16)


def running(logs):
    first, rest = split(logs)
    second, third = split(logs - first.astype(F32))
    upper = lax.broadcasted_iota(jnp.int32, (T, T), 0) <= lax.broadcasted_iota(jnp.int32, (T, T), 1)
    ones = jnp.where(upper, 1.0, 0.0).astype(BF16)
    return dot(first, ones) + (dot(second, ones) + dot(third, ones))


def rows(per_head):
    heads, lanes = per_head.shape
    spread = jnp.broadcast_to(per_head[:, None, :], (heads, HEAD, lanes))
    return spread.reshape(heads * HEAD, lanes)


def column(logs, token):
    return jnp.broadcast_to(logs[:, token : token + 1], logs.shape)


def chunk_logs(logs_ref, number):
    return block_logs(logs_ref[:, number * T : (number + 1) * T])


def block_logs(logs):
    sums = running(logs)
    return sums, column(sums, MID), column(sums, T - 1)


def tokens_of(ref, number):
    return ref[number * T : (number + 1) * T, :]


def lanes_at(ref, number):
    return ref.at[:, number * T : (number + 1) * T]


def tokens_at(ref, number, count=T):
    return ref.at[number * count : (number + 1) * count, :]


def start_copies(pairs, sems, first=0):
    copies = [pltpu.make_async_copy(source, target, sems.at[first + n]) for n, (source, target) in enumerate(pairs)]
    for copy in copies:
        copy.start()
    return copies


def wait_all(copies):
    for copy in copies:
        copy.wait()


def lanes_of(ref, number):
    return ref[:, number * T : (number + 1) * T]


def chunk_pairs(hbm_ref, ref, order):
    return [(hbm_ref.at[n], ref.at[n]) for n in order]


def live_mask(number, length, width):
    token = lax.broadcasted_iota(jnp.int32, (width, T), 1) + number * T
    return token < length


def twice(value):
    return jnp.concatenate([value, value], axis=0)


def side(left, right):
    return jnp.concatenate([left, right], axis=1)


def own_group(ref, group, all_ref):
    all_ref[...] = ref.astype(F32)
    return all_ref[pl.ds(group, T, stride=GROUPS), :].astype(BF16)


def ends_kernel(
    length_ref, group_ref, cot_hbm, logs_hbm, key_hbm, query_hbm, ends_hbm, own_key_hbm, own_query_hbm, start_ref,
    cot_ref, logs_ref, ends_ref, own_key_ref, own_query_ref, raw_k, raw_q, all_k, all_q, sems,
):
    chunks, width = ends_ref.shape[0], ends_ref.shape[1]
    order = list(range(chunks - 1, -1, -1))
    raw_pairs = [(tokens_at(query_hbm, n, T * GROUPS), raw_q.at[n]) for n in order]
    pairs = [(logs_hbm, logs_ref), (cot_hbm, cot_ref)] + raw_pairs
    pairs += [(tokens_at(key_hbm, n, T * GROUPS), raw_k.at[n]) for n in order]
    copies = start_copies(pairs, sems)
    wait_all(copies[:2])
    current = jnp.zeros((width, N), F32)
    sent = []
    for step, n in enumerate(order):
        copies[2 + step].wait()
        queries = own_group(raw_q[n], group_ref[0], all_q.at[step % 2])
        own_query_ref[n * T : (n + 1) * T, :] = queries
        sums, mid, last = chunk_logs(logs_ref, n)
        scaled = lanes_of(cot_ref, n).astype(F32) * rows(jnp.exp(sums - mid))
        scaled = jnp.where(live_mask(n, length_ref[0], width), scaled, 0.0)
        high, low = split(scaled)
        pulled = dot(side(high, low), twice(queries))
        ends_ref[n] = current
        sent += start_copies([(ends_ref.at[n], ends_hbm.at[n])], sems, len(copies) + step)
        current = rows(jnp.exp(last)) * current + rows(jnp.exp(mid)) * pulled
    start_ref[...] = current
    for step, n in enumerate(order):
        copies[2 + chunks + step].wait()
        own_key_ref[n * T : (n + 1) * T, :] = own_group(raw_k[n], group_ref[0], all_k.at[step % 2])
    pairs = [(own_key_ref, own_key_hbm), (own_query_ref, own_query_hbm)]
    wait_all(sent + start_copies(pairs, sems, len(copies) + chunks))


PLANES = 8


def half_rows(place, core):
    return pl.multiple_of((place // PLANES) * 8 * HEAD + core * 4 * HEAD + (place % PLANES) * PART, PART)


def summary_kernel(
    core_ref, input_hbm, cot_hbm, logs_hbm, key_hbm, query_hbm,
    carried_hbm, pulled_hbm, mine_ref, peer_ref, total_ref,
    input_ref, cot_ref, logs_ref, key_ref, query_ref, carried_ref, pulled_ref, all_c, all_p, sems,
):
    chunks = carried_ref.shape[0]
    order = range(chunks)
    pairs = [
        (logs_hbm, logs_ref), (key_hbm, key_ref), (input_hbm, input_ref), (query_hbm, query_ref), (cot_hbm, cot_ref)
    ]
    copies = start_copies(pairs, sems)
    wait_all(copies[:3])
    total = jnp.zeros(total_ref.shape, F32)
    sent = []
    for n in order:
        sums, mid, last = chunk_logs(logs_ref, n)
        high, low = split(lanes_of(input_ref, n).astype(F32) * rows(jnp.exp(mid - sums)))
        carried = dot(side(high, low), twice(tokens_of(key_ref, n)))
        carried = rows(jnp.exp(last - mid)) * carried
        carried_ref[n] = carried
        sent += start_copies([(carried_ref.at[n], carried_hbm.at[n])], sems, len(copies) + 2 * n)
        all_c[...] = carried if n == 0 else rows(jnp.exp(last)) * all_c[...] + carried
        if n == 0:
            wait_all(copies[3:])
        high, low = split(lanes_of(cot_ref, n).astype(F32) * rows(jnp.exp(sums - mid)))
        pulled = dot(side(high, low), twice(tokens_of(query_ref, n)))
        pulled = rows(jnp.exp(mid)) * pulled
        pulled_ref[n] = pulled
        sent += start_copies([(pulled_ref.at[n], pulled_hbm.at[n])], sems, len(copies) + 2 * n + 1)
        all_p[...] = pulled if n == 0 else all_p[...] + rows(jnp.exp(total)) * pulled
        total = total + last
    total_ref[...] = total
    core = core_ref[0]
    places = mine_ref.shape[0]
    for place in range(places):
        for ref, side_core in ((mine_ref, core), (peer_ref, 1 - core)):
            here = pl.ds(half_rows(place, side_core), PART)
            ref[place, :PART] = all_c[here, :]
            ref[place, PART:] = all_p[here, :]
    heads = total_ref.shape[0]
    peer_ref[places, :heads] = total_ref[...]
    peer_ref[places, heads:] = jnp.zeros_like(peer_ref[places, heads:])
    wait_all(sent)


def both_totals(first, head, mine_ref, got_ref):
    mine = mine_ref[pl.ds(head, 1), :]
    theirs = got_ref[got_ref.shape[0] - 1, pl.ds(head, 1), :]
    return jnp.where(first, mine, theirs), jnp.where(first, theirs, mine)


STATES = 2 * PART
GRADS = STATES + 8


def head_of(place, side_y, core):
    return side_y * 8 + core * 4 + place * PART // HEAD


def joined(first, mine, theirs, total0, total1):
    zero, one = jnp.where(first, mine, theirs), jnp.where(first, theirs, mine)
    return jnp.exp(total1) * zero[:PART] + one[:PART], zero[PART:] + jnp.exp(total0) * one[PART:]


def parted(first, mine, theirs, total0, total1, start, end):
    carried0 = jnp.where(first, mine[:PART], theirs[:PART])
    pulled1 = jnp.where(first, theirs[PART:], mine[PART:])
    start1 = jnp.exp(total0) * start + carried0
    end0 = jnp.exp(total1) * end + pulled1
    own = jnp.where(first, start, start1), jnp.where(first, end0, end)
    return own, (jnp.where(first, start1, start), jnp.where(first, end, end0))


def pack_chip_kernel(at_ref, mine_ref, got_ref, total_ref, keep_ref, away_ref, chip_total_ref):
    core, y = at_ref[0], at_ref[1]
    heads = total_ref.shape[0]
    chip_total_ref[...] = total_ref[...] + got_ref[got_ref.shape[0] - 1, :heads]
    for place in range(PLANES):
        for ref, side_y in ((keep_ref, y), (away_ref, 1 - y)):
            total0, total1 = both_totals(core == 0, head_of(place, side_y, core), total_ref, got_ref)
            here = side_y * PLANES + place
            carried, pulled = joined(core == 0, mine_ref[here], got_ref[here], total0, total1)
            ref[place, :PART] = carried
            ref[place, PART:] = pulled
    away_ref[PLANES, :heads] = chip_total_ref[...]
    away_ref[PLANES, heads:] = jnp.zeros_like(away_ref[PLANES, heads:])


def pack_kernel(at_ref, keep_ref, got_ref, total_ref, start_ref, out_ref):
    core, y = at_ref[0], at_ref[1]
    for place in range(PLANES):
        total0, total1 = both_totals(y == 0, head_of(place, y, core), total_ref, got_ref)
        carried, pulled = joined(y == 0, keep_ref[place], got_ref[place], total0, total1)
        out_ref[place, :PART] = carried
        out_ref[place, PART:STATES] = pulled
        out_ref[place, STATES:GRADS] = jnp.broadcast_to(total0 + total1, (8, N))
        out_ref[place, GRADS:] = start_ref[PART * place : PART * (place + 1)]


def scan_kernel(blocks_ref, starts_ref, out_ref):
    current = jnp.zeros((PART, N), F32)
    for place in range(PLANES):
        starts_ref[place] = current
        current = jnp.exp(blocks_ref[place, STATES : STATES + 1]) * current + blocks_ref[place, :PART]
    for group in range(out_ref.shape[0]):
        out_ref[group, :PART] = blocks_ref[group, GRADS:]
        out_ref[group, PART:] = current


def scan_back_kernel(blocks_ref, starts_ref, got_ref, out_ref):
    current = got_ref[0, :PART]
    for answer in range(1, got_ref.shape[0]):
        current = current + got_ref[answer, :PART]
    for place in range(PLANES - 1, -1, -1):
        out_ref[place, :PART] = starts_ref[place]
        out_ref[place, PART:STATES] = current
        out_ref[place, STATES:] = got_ref[place, PART:]
        current = jnp.exp(blocks_ref[place, STATES : STATES + 1]) * current + blocks_ref[place, PART:STATES]


def unpack_kernel(at_ref, keep_ref, got_ref, total_ref, states_ref, own_ref, other_ref):
    core, y = at_ref[0], at_ref[1]
    for place in range(PLANES):
        total0, total1 = both_totals(y == 0, head_of(place, y, core), total_ref, got_ref)
        own, other = parted(
            y == 0, keep_ref[place], got_ref[place], total0, total1,
            states_ref[place, :PART], states_ref[place, PART:STATES],
        )
        for ref, (start, end) in ((own_ref, own), (other_ref, other)):
            ref[place, :PART] = start
            ref[place, PART:] = end


def unpack_chip_kernel(at_ref, mine_ref, got_ref, total_ref, near_ref, away_ref, own_ref, other_ref):
    core, y = at_ref[0], at_ref[1]
    for place in range(PLANES):
        for chip_ref, side_y in ((near_ref, y), (away_ref, 1 - y)):
            total0, total1 = both_totals(core == 0, head_of(place, side_y, core), total_ref, got_ref)
            here = side_y * PLANES + place
            own, other = parted(
                core == 0, mine_ref[here], got_ref[here], total0, total1,
                chip_ref[place, :PART], chip_ref[place, PART:],
            )
            for ref, (start, end) in ((own_ref, own), (other_ref, other)):
                ref[here, :PART] = start
                ref[here, PART:] = end


def gather_kernel(parts_ref, key_ref, query_ref, sums_ref):
    for ref, first in ((key_ref, 0), (query_ref, PART)):
        for group in range(GROUPS):
            chip0, chip1 = parts_ref[2 * group], parts_ref[2 * group + 1]
            sums_ref[pl.ds(group, PART, stride=GROUPS), :] = (chip0 + chip1)[first : first + PART]
        ref[...] = sums_ref[...].astype(BF16)


def chunk_grads(inputs, cot, logs3, keys, queries, start, end):
    sums, mid, last = logs3
    grow = rows(jnp.exp(mid - sums))
    fall = rows(jnp.exp(sums - mid))
    in_high, in_low = split(inputs * grow)
    cot_high, cot_low = split(cot * fall)
    end_high, end_low = split(rows(jnp.exp(last - mid)) * end)
    start_high, start_low = split(rows(jnp.exp(mid)) * start)
    first = lax.broadcasted_iota(jnp.int32, (T, T), 0)
    second = lax.broadcasted_iota(jnp.int32, (T, T), 1)
    score_high, score_low = split(jnp.where(first >= second, dot_nt(queries, keys), 0.0))
    input_grad = dot(side(cot_high, cot_low), twice(score_high)) + dot(cot_high, score_low)
    input_grad = input_grad + dot_nt(side(end_high, end_low), side(keys, keys))
    input_grad = grow * input_grad
    in_high_t, in_low_t = in_high.T, in_low.T
    right_high, right_low = side(cot_high, end_high), side(cot_low, end_low)
    both = dot(in_high_t, right_high) + (dot(in_high_t, right_low) + dot(in_low_t, right_high))
    products = jnp.where(second >= first, both[:, :T], 0.0)
    high, low = split(products)
    key_grad = both[:, T:] + dot(side(high, low), twice(queries))
    high, low = split(products.T)
    query_grad = dot(side(high, low), twice(keys))
    cot_high_t, cot_low_t = cot_high.T, cot_low.T
    query_grad = query_grad + dot(cot_high_t, start_high)
    query_grad = query_grad + (dot(cot_high_t, start_low) + dot(cot_low_t, start_high))
    return input_grad, key_grad, query_grad, (in_high, in_low)


def by_core(number, core, value, mine_ref, peer_ref):
    value = value.reshape(2, 2, PART, N)
    here = pl.ds(2 * number, 2)
    mine_ref[here] = jnp.where(core == 0, value[:, 0], value[:, 1])
    peer_ref[here] = jnp.where(core == 0, value[:, 1], value[:, 0])


def answer_kernel(
    length_ref, core_ref, input_hbm, cot_hbm, logs_hbm, key_hbm, query_hbm, ends_hbm,
    input_grad_hbm, query_grad_hbm, key_mine_ref, key_peer_ref,
    input_ref, cot_ref, logs_ref, key_ref, query_ref, ends_ref, input_grad_ref, query_grad_ref, state_ref, sems,
):
    chunks, width = ends_ref.shape[0], ends_ref.shape[1]
    order = range(chunks)
    pairs = [
        (logs_hbm, logs_ref), (key_hbm, key_ref), (query_hbm, query_ref), (input_hbm, input_ref), (cot_hbm, cot_ref)
    ]
    copies = start_copies(pairs + chunk_pairs(ends_hbm, ends_ref, order), sems)
    wait_all(copies[:5])
    state_ref[...] = jnp.zeros_like(state_ref)
    sent = []
    for n in order:
        logs3 = chunk_logs(logs_ref, n)
        sums, mid, last = logs3
        copies[5 + n].wait()
        cot = jnp.where(live_mask(n, length_ref[0], width), lanes_of(cot_ref, n).astype(F32), 0.0)
        keys, queries = tokens_of(key_ref, n), tokens_of(query_ref, n)
        start = state_ref[...]
        input_grad, key_grad, query_grad, (high, low) = chunk_grads(
            lanes_of(input_ref, n).astype(F32), cot, logs3, keys, queries, start, ends_ref[n]
        )
        input_grad_ref[n] = input_grad.astype(BF16)
        by_core(n, core_ref[0], key_grad, key_mine_ref, key_peer_ref)
        query_grad_ref[n * T : (n + 1) * T, :] = query_grad
        pairs = [
            (input_grad_ref.at[n], lanes_at(input_grad_hbm, n)),
            (tokens_at(query_grad_ref, n), tokens_at(query_grad_hbm, n)),
        ]
        sent += start_copies(pairs, sems, len(copies) + 2 * n)
        carried = dot(side(high, low), twice(keys))
        state_ref[...] = rows(jnp.exp(last)) * start + rows(jnp.exp(last - mid)) * carried
    wait_all(sent)


def prompt_near_kernel(
    input_hbm, cot_hbm, logs_hbm, key_hbm, query_hbm, input_grad_hbm, key_grad_hbm, query_grad_hbm,
    input_ref, cot_ref, logs_ref, key_ref, query_ref, input_grad_ref, key_grad_ref, query_grad_ref, sems,
):
    first = lax.broadcasted_iota(jnp.int32, (T, T), 0)
    second = lax.broadcasted_iota(jnp.int32, (T, T), 1)
    order = range(input_ref.shape[1] // T)
    pairs = [
        (logs_hbm, logs_ref), (key_hbm, key_ref), (query_hbm, query_ref), (input_hbm, input_ref), (cot_hbm, cot_ref)
    ]
    copies = start_copies(pairs, sems)
    wait_all(copies)
    sent = []
    for n in order:
        here = slice(n * T, (n + 1) * T)
        sums, mid, _ = chunk_logs(logs_ref, n)
        keys, queries = tokens_of(key_ref, n), tokens_of(query_ref, n)
        grow = rows(jnp.exp(mid - sums))
        in_high, in_low = split(lanes_of(input_ref, n).astype(F32) * grow)
        cot_high, cot_low = split(lanes_of(cot_ref, n).astype(F32) * rows(jnp.exp(sums - mid)))
        score_high, score_low = split(jnp.where(first >= second, dot_nt(queries, keys), 0.0))
        input_grad = dot(side(cot_high, cot_low), twice(score_high)) + dot(cot_high, score_low)
        input_grad_ref[n] = grow * input_grad
        in_high_t, in_low_t = in_high.T, in_low.T
        both = dot(in_high_t, side(cot_high, cot_low))
        products = both[:, :T] + (both[:, T:] + dot(in_low_t, cot_high))
        products = jnp.where(second >= first, products, 0.0)
        high, low = split(products)
        key_grad_ref[here, :] = dot(side(high, low), twice(queries))
        high, low = split(products.T)
        query_grad_ref[here, :] = dot(side(high, low), twice(keys))
        pairs = [
            (input_grad_ref.at[n], input_grad_hbm.at[n]),
            (tokens_at(key_grad_ref, n), tokens_at(key_grad_hbm, n)),
            (tokens_at(query_grad_ref, n), tokens_at(query_grad_hbm, n)),
        ]
        sent += start_copies(pairs, sems, len(copies) + 3 * n)
    wait_all(sent)


def prompt_far_kernel(
    core_ref, input_hbm, cot_hbm, logs_hbm, key_hbm, carried_hbm, pulled_hbm,
    near_input_hbm, near_key_hbm, near_query_hbm, own_hbm, got_hbm,
    input_grad_hbm, key_grad_hbm, query_grad_hbm,
    input_ref, cot_ref, logs_ref, key_ref, carried_ref, pulled_ref, near_input_ref, near_key_ref, near_query_ref,
    own_ref, got_ref, input_grad_ref, key_grad_ref, query_grad_ref, end_ref, start_ref, sems,
):
    chunks = carried_ref.shape[0]
    core = core_ref[0]
    order = range(chunks)
    pairs = [
        (own_hbm, own_ref), (got_hbm, got_ref), (logs_hbm, logs_ref), (key_hbm, key_ref), (input_hbm, input_ref),
        (cot_hbm, cot_ref), (near_key_hbm, near_key_ref), (near_query_hbm, near_query_ref),
    ]
    first = len(pairs)
    for three in zip(
        chunk_pairs(near_input_hbm, near_input_ref, order[::-1]), chunk_pairs(pulled_hbm, pulled_ref, order[::-1]),
        chunk_pairs(carried_hbm, carried_ref, order),
    ):
        pairs += three
    copies = start_copies(pairs, sems)
    wait_all(copies[:2])
    for place in range(own_ref.shape[0]):
        for ref, side_core in ((own_ref, core), (got_ref, 1 - core)):
            here = pl.ds(half_rows(place, side_core), PART)
            start_ref[here, :] = ref[place, :PART]
            end_ref[here, :] = ref[place, PART:]
    wait_all(copies[2:first])
    sent = []
    for step in range(chunks):
        wait_all(copies[first + 3 * step : first + 3 * step + 3])
        n = chunks - 1 - step
        here = slice(n * T, (n + 1) * T)
        sums, mid, last = chunk_logs(logs_ref, n)
        end = end_ref[...]
        end_ref[...] = rows(jnp.exp(last)) * end + pulled_ref[n]
        keys = tokens_of(key_ref, n)
        grow = rows(jnp.exp(mid - sums))
        in_high, in_low = split(lanes_of(input_ref, n).astype(F32) * grow)
        end_high, end_low = split(rows(jnp.exp(last - mid)) * end)
        input_grad = dot_nt(side(end_high, end_low), side(keys, keys))
        input_grad_ref[n] = (near_input_ref[n] + grow * input_grad).astype(BF16)
        pairs = [(input_grad_ref.at[n], lanes_at(input_grad_hbm, n))]
        sent += start_copies(pairs, sems, len(copies) + 3 * step)
        in_high_t, in_low_t = in_high.T, in_low.T
        both = dot(in_high_t, side(end_high, end_low))
        key_grad = both[:, :N] + (both[:, N:] + dot(in_low_t, end_high))
        key_grad_ref[here, :] = (near_key_ref[here, :] + key_grad).astype(BF16)
        pairs = [(tokens_at(key_grad_ref, n), tokens_at(key_grad_hbm, n))]
        sent += start_copies(pairs, sems, len(copies) + 3 * step + 1)

        n = step
        here = slice(n * T, (n + 1) * T)
        sums, mid, last = chunk_logs(logs_ref, n)
        start = start_ref[...]
        start_ref[...] = rows(jnp.exp(last)) * start + carried_ref[n]
        cot_high, cot_low = split(lanes_of(cot_ref, n).astype(F32) * rows(jnp.exp(sums - mid)))
        start_high, start_low = split(rows(jnp.exp(mid)) * start)
        cot_high_t, cot_low_t = cot_high.T, cot_low.T
        both = dot(cot_high_t, side(start_high, start_low))
        query_grad = both[:, :N] + (both[:, N:] + dot(cot_low_t, start_high))
        query_grad_ref[here, :] = (near_query_ref[here, :] + query_grad).astype(BF16)
        pairs = [(tokens_at(query_grad_ref, n), tokens_at(query_grad_hbm, n))]
        sent += start_copies(pairs, sems, len(copies) + 3 * step + 2)
    wait_all(sent)


def prepare_kernel(length_ref, cot_ref, logs_ref, local_ref, high_ref, low_ref, local_out_ref):
    local_out_ref[...] = local_ref[...]
    total = jnp.zeros((logs_ref.shape[0], T), F32)
    for n in range(cot_ref.shape[1] // T):
        sums, _, last = chunk_logs(logs_ref, n)
        scaled = lanes_of(cot_ref, n).astype(F32) * rows(jnp.exp(total + sums))
        scaled = jnp.where(live_mask(n, length_ref[0], cot_ref.shape[0]), scaled, 0.0)
        high, low = split(scaled)
        high_ref[n * T : (n + 1) * T, :] = high.T
        low_ref[n * T : (n + 1) * T, :] = low.T
        total = total + last


def start_part_kernel(core_ref, high_ref, low_ref, local_ref, state_ref, mine_ref, peer_ref):
    state = jnp.concatenate([state_ref[place, STATES:] for place in range(state_ref.shape[0])], axis=0)
    state_high, state_low = split(state)
    both = side(state_high, state_low)
    for n in range(high_ref.shape[0] // T):
        part = dot(tokens_of(high_ref, n), both)
        part = part[:, :N] + (part[:, N:] + dot(tokens_of(low_ref, n), state_high))
        by_core(n, core_ref[0], tokens_of(local_ref, n) + part, mine_ref, peer_ref)


def tail_kernel(key_ref, query_mine_ref, query_got_ref, out_ref):
    out_ref[:, :PART] = key_ref[...]
    out_ref[:, PART:] = query_mine_ref[...] + query_got_ref[...]


def shape(*dims, dtype=F32):
    return jax.ShapeDtypeStruct(dims, dtype)


IN_HBM = pl.BlockSpec(memory_space=pltpu.HBM)
IN_VMEM = pl.BlockSpec(memory_space=pltpu.VMEM)


def held(*dims, dtype=F32):
    return pltpu.VMEM(dims, dtype)


def loading(kernel, scalars, far, outs):
    def run(*refs):
        first, sources, rest = refs[:scalars], refs[scalars : scalars + far], refs[scalars + far :]
        *rest, sems = rest
        targets, rest = rest[len(rest) - far :], rest[: len(rest) - far]
        wait_all(start_copies(list(zip(sources, targets)), sems))
        kernel(*first, *targets, *rest)

    return run


def call(kernel, outs, scratch=(), copies=0, scalars=0, far=0, count=0, far_outs=0, flops=0, name=None):
    def run(*args):
        sems, extra, inner = copies, [], kernel
        if far and not copies:
            sources = args[scalars : scalars + far]
            extra = [pltpu.VMEM(source.shape, source.dtype) for source in sources]
            sems, inner = far, loading(kernel, scalars, far, outs)
        return pl.pallas_call(
            inner,
            out_shape=outs,
            in_specs=[pl.BlockSpec(memory_space=pltpu.SMEM)] * scalars + [IN_HBM] * far + [IN_VMEM] * count,
            out_specs=[IN_HBM] * far_outs + [IN_VMEM] * (len(outs) - far_outs),
            scratch_shapes=list(scratch) + extra + ([pltpu.SemaphoreType.DMA((sems,))] if sems else []),
            compiler_params=pltpu.CompilerParams(vmem_limit_bytes=LARGE if sems else SMALL),
            cost_estimate=pl.CostEstimate(flops=flops, bytes_accessed=2000000, transcendentals=0),
            name=name,
        )(*args)

    return run


def body(
    prompt_inputs, prompt_keys, prompt_queries, prompt_logdecay, prompt_cotangent,
    answer_inputs, answer_keys, answer_queries, answer_logdecay, answer_cotangent, answer_lengths,
):
    tokens, heads, _ = prompt_inputs.shape
    _, length, answer_heads, _ = answer_inputs.shape
    width, answer_width = heads * HEAD, answer_heads * HEAD
    chunks, answer_chunks = tokens // T, length // T
    seq, comp = lax.axis_size("seq"), lax.axis_size("comp")
    quads = heads // answer_heads
    planes = seq // quads
    chips = seq // 2
    same_core = [[2 * chip + side for chip in range(chips)] for side in range(2)]
    same_pair = [[quads * plane + q for plane in range(planes)] for q in range(quads)]
    place = lax.axis_index("seq").astype(jnp.int32)
    group = (place // quads).reshape(1)
    core, y = place % 2, place // 2 % 2
    at = jnp.stack([core, y])
    core = core.reshape(1)

    def swap_cores(value):
        return lax.ppermute(value, "seq", [(i, i ^ 1) for i in range(seq)])

    def swap_chips(value):
        return lax.ppermute(value, "seq", [(i, i ^ 2) for i in range(seq)])

    def over(value, axis, groups=None):
        return lax.all_to_all(value, axis, 0, 0, axis_index_groups=groups, tiled=True)

    x = jnp.transpose(prompt_inputs, (1, 2, 0)).reshape(width, tokens)
    cot = jnp.transpose(prompt_cotangent, (1, 2, 0)).reshape(width, tokens)
    logs = prompt_logdecay.T
    keys, queries = prompt_keys.reshape(tokens, N), prompt_queries.reshape(tokens, N)
    ax = jnp.transpose(answer_inputs[0], (1, 2, 0)).reshape(answer_width, length)
    acot = jnp.transpose(answer_cotangent[0], (1, 2, 0)).reshape(answer_width, length)
    alogs = answer_logdecay[0].T
    all_keys, all_queries = answer_keys.reshape(length * GROUPS, N), answer_queries.reshape(length * GROUPS, N)

    prompt_lanes, prompt_rows = held(width, tokens, dtype=BF16), held(tokens, N, dtype=BF16)
    prompt_states = held(chunks, width, N)
    prompt_scratch = [prompt_lanes, prompt_lanes, held(heads, tokens), prompt_rows, prompt_rows]
    carried, pulled, mine, peer, totals = call(
        summary_kernel,
        [
            shape(chunks, width, N), shape(chunks, width, N), shape(chips, 2 * PART, N),
            shape(chips + 1, 2 * PART, N), shape(heads, N),
        ],
        scratch=prompt_scratch + [prompt_states, prompt_states, held(width, N), held(width, N)],
        copies=5 + 2 * chunks, scalars=1, far=5, far_outs=2, flops=10**9, name="prompt_summary",
    )(core, x, cot, logs, keys, queries)
    theirs = swap_cores(peer)

    answer_lanes, answer_rows = held(answer_width, length, dtype=BF16), held(length, N, dtype=BF16)
    answer_logs, answer_states = held(answer_heads, length), held(answer_chunks, answer_width, N)
    raw, raw_chunk = held(answer_chunks, T * GROUPS, N, dtype=BF16), held(2, T * GROUPS, N)
    ends, akeys, aqueries, start_grad = call(
        ends_kernel,
        [
            shape(answer_chunks, answer_width, N), shape(length, N, dtype=BF16), shape(length, N, dtype=BF16),
            shape(answer_width, N),
        ],
        scratch=[answer_lanes, answer_logs, answer_states, answer_rows, answer_rows, raw, raw, raw_chunk, raw_chunk],
        copies=4 + 3 * answer_chunks, scalars=2, far=4, far_outs=3, flops=10**9, name="answer_ends",
    )(answer_lengths, group, acot, alogs, all_keys, all_queries)
    half = shape(planes, 2 * PART, N)
    half_more = shape(planes + 1, 2 * PART, N)
    keep, away, chip_totals = call(
        pack_chip_kernel, [half, half_more, shape(heads, N)], scalars=1, count=3, flops=10**7, name="pack_chip"
    )(at, mine, theirs, totals)
    chip_theirs = swap_chips(away)
    (sent,) = call(
        pack_kernel, [shape(planes, GRADS + PART, N)], scalars=1, count=4, flops=10**7, name="pack"
    )(at, keep, chip_theirs, chip_totals, start_grad)
    blocks = over(sent, "seq", same_pair)

    near_input, near_key, near_query = call(
        prompt_near_kernel, [shape(chunks, width, T), shape(tokens, N), shape(tokens, N)],
        scratch=prompt_scratch + [held(chunks, width, T), held(tokens, N), held(tokens, N)],
        copies=5 + 3 * chunks, far=5, far_outs=3, flops=3 * 10**9, name="prompt_near",
    )(x, cot, logs, keys, queries)
    ax_grad, aq_local, key_mine, key_peer = call(
        answer_kernel,
        [
            shape(answer_width, length, dtype=BF16), shape(length, N),
            shape(chips, PART, N), shape(chips, PART, N),
        ],
        scratch=[
            answer_lanes, answer_lanes, answer_logs, answer_rows, answer_rows, answer_states,
            held(answer_chunks, answer_width, T, dtype=BF16), held(length, N), held(answer_width, N),
        ],
        copies=5 + 3 * answer_chunks, scalars=2, far=6, far_outs=2, flops=3 * 10**9, name="answer_grads",
    )(answer_lengths, core, ax, acot, alogs, akeys, aqueries, ends)

    starts, sent = call(
        scan_kernel, [shape(planes, PART, N), shape(comp, 2 * PART, N)], count=1, flops=10**7, name="scan"
    )(blocks)
    sent, ax_grad, aq_local, key_mine, key_peer = lax.optimization_barrier(
        (sent, ax_grad, aq_local, key_mine, key_peer)
    )
    finals = over(sent, "comp")
    key_parts = key_mine + swap_cores(key_peer)
    finals, near_input, near_key, near_query = lax.optimization_barrier((finals, near_input, near_key, near_query))
    (sent,) = call(
        scan_back_kernel, [shape(planes, 3 * PART, N)], count=3, flops=10**7, name="scan_back"
    )(blocks, starts, finals)
    sent, late_cot, late_logs, aq_local = lax.optimization_barrier((sent, acot, alogs, aq_local))
    states = over(sent, "seq", same_pair)
    late_high, late_low, aq_local = call(
        prepare_kernel,
        [shape(length, answer_width, dtype=BF16), shape(length, answer_width, dtype=BF16), shape(length, N)],
        scalars=1, count=3, flops=10**9, name="answer_prepare",
    )(answer_lengths, late_cot, late_logs, aq_local)
    chip_own, chip_other = call(
        unpack_kernel, [half, half], scalars=1, count=4, flops=10**7, name="unpack"
    )(at, keep, chip_theirs, chip_totals, states)
    states, chip_own, chip_other = lax.optimization_barrier((states, chip_own, chip_other))
    chip_got = swap_chips(chip_other)

    query_mine, query_peer = call(
        start_part_kernel, [shape(chips, PART, N), shape(chips, PART, N)],
        scalars=1, count=4, flops=10**9, name="answer_start_part",
    )(core, late_high, late_low, aq_local, states)
    (sent,) = call(tail_kernel, [shape(chips, 2 * PART, N)], count=3, flops=10**7, name="pack_tail")(
        key_parts, query_mine, swap_cores(query_peer)
    )
    parts = over(sent, "seq", same_core)
    own, other = call(
        unpack_chip_kernel, [shape(chips, 2 * PART, N), shape(chips, 2 * PART, N)],
        scalars=1, count=5, flops=10**7, name="unpack_chip",
    )(at, mine, theirs, totals, chip_own, chip_got)
    x_grad, k_grad, q_grad = call(
        prompt_far_kernel,
        [shape(width, tokens, dtype=BF16), shape(tokens, N, dtype=BF16), shape(tokens, N, dtype=BF16)],
        scratch=[
            prompt_lanes, prompt_lanes, held(heads, tokens), prompt_rows, prompt_states, prompt_states,
            held(chunks, width, T), held(tokens, N), held(tokens, N),
            held(chips, 2 * PART, N), held(chips, 2 * PART, N),
            held(chunks, width, T, dtype=BF16), prompt_rows, prompt_rows, held(width, N), held(width, N),
        ],
        copies=8 + 6 * chunks, scalars=1, far=11, far_outs=3, flops=3 * 10**9, name="prompt_far",
    )(
        core, x, cot, logs, keys, carried, pulled, near_input, near_key, near_query, own, swap_cores(other),
    )

    parts, x_grad, k_grad, q_grad = lax.optimization_barrier((parts, x_grad, k_grad, q_grad))
    gathered = shape(PART * GROUPS, N, dtype=BF16)
    key_out, query_out = call(
        gather_kernel, [gathered, gathered], scratch=[held(PART * GROUPS, N)],
        count=1, flops=10**7, name="gather_groups",
    )(parts)

    return (
        jnp.transpose(x_grad.reshape(heads, HEAD, tokens), (2, 0, 1)),
        k_grad.reshape(tokens, 1, N),
        q_grad.reshape(tokens, 1, N),
        jnp.transpose(ax_grad.reshape(answer_heads, HEAD, length), (2, 0, 1))[None],
        key_out.reshape(1, PART, GROUPS, N),
        query_out.reshape(1, PART, GROUPS, N),
    )


def solution(mesh):
    in_specs = (
        P("seq", "comp", None),
        P("seq", "comp", None),
        P("seq", "comp", None),
        P("seq", "comp"),
        P("seq", "comp", None),
        P("comp", None, "seq", None),
        P("comp", None, None, None),
        P("comp", None, None, None),
        P("comp", None, "seq"),
        P("comp", None, "seq", None),
        P("comp"),
    )
    out_specs = (
        P("seq", "comp", None),
        P("seq", "comp", None),
        P("seq", "comp", None),
        P("comp", None, "seq", None),
        P("comp", "seq", None, None),
        P("comp", "seq", None, None),
    )
    return jax.shard_map(body, mesh=mesh, in_specs=in_specs, out_specs=out_specs, check_vma=False)
```

```python
import functools

import jax
import jax.numpy as jnp
from jax import lax
from jax.experimental import pallas as pl
from jax.experimental.pallas import tpu as pltpu
from jax.sharding import PartitionSpec as P

F32 = jnp.float32
BF16 = jnp.bfloat16
T = 128
MID = 63
N = 128
GROUPS = 8
HEAD = 64
PART = 32
SMALL, LARGE = 16 * 1024 * 1024, 56 * 1024 * 1024


def dot(left, right):
    return lax.dot_general(left, right, (((1,), (0,)), ((), ())), preferred_element_type=F32)


def dot_nt(left, right):
    return lax.dot_general(left, right, (((1,), (1,)), ((), ())), preferred_element_type=F32)


def split(value):
    high = value.astype(BF16)
    return high, (value - high.astype(F32)).astype(BF16)


def running(logs):
    first, rest = split(logs)
    second, third = split(logs - first.astype(F32))
    upper = lax.broadcasted_iota(jnp.int32, (T, T), 0) <= lax.broadcasted_iota(jnp.int32, (T, T), 1)
    ones = jnp.where(upper, 1.0, 0.0).astype(BF16)
    return dot(first, ones) + (dot(second, ones) + dot(third, ones))


def rows(per_head):
    heads, lanes = per_head.shape
    spread = jnp.broadcast_to(per_head[:, None, :], (heads, HEAD, lanes))
    return spread.reshape(heads * HEAD, lanes)


def column(logs, token):
    return jnp.broadcast_to(logs[:, token : token + 1], logs.shape)


def chunk_logs(logs_ref, number):
    return block_logs(logs_ref[:, number * T : (number + 1) * T])


def block_logs(logs):
    sums = running(logs)
    return sums, column(sums, MID), column(sums, T - 1)


def tokens_of(ref, number):
    return ref[number * T : (number + 1) * T, :]


def lanes_at(ref, number):
    return ref.at[:, number * T : (number + 1) * T]


def tokens_at(ref, number, count=T):
    return ref.at[number * count : (number + 1) * count, :]


def start_copies(pairs, sems, first=0):
    copies = [pltpu.make_async_copy(source, target, sems.at[first + n]) for n, (source, target) in enumerate(pairs)]
    for copy in copies:
        copy.start()
    return copies


def wait_all(copies):
    for copy in copies:
        copy.wait()


def lanes_of(ref, number):
    return ref[:, number * T : (number + 1) * T]


def chunk_pairs(hbm_ref, ref, order):
    return [(hbm_ref.at[n], ref.at[n]) for n in order]


def live_mask(number, length, width):
    token = lax.broadcasted_iota(jnp.int32, (width, T), 1) + number * T
    return token < length


def twice(value):
    return jnp.concatenate([value, value], axis=0)


def side(left, right):
    return jnp.concatenate([left, right], axis=1)


def own_group(ref, group, all_ref):
    all_ref[...] = ref.astype(F32)
    return all_ref[pl.ds(group, T, stride=GROUPS), :].astype(BF16)


def ends_kernel(
    length_ref, group_ref, cot_hbm, logs_hbm, key_hbm, query_hbm, ends_hbm, own_key_hbm, own_query_hbm, start_ref,
    cot_ref, logs_ref, ends_ref, own_key_ref, own_query_ref, raw_k, raw_q, all_k, all_q, sems,
):
    chunks, width = ends_ref.shape[0], ends_ref.shape[1]
    order = list(range(chunks - 1, -1, -1))
    raw_pairs = [(tokens_at(query_hbm, n, T * GROUPS), raw_q.at[n]) for n in order]
    pairs = [(logs_hbm, logs_ref), (cot_hbm, cot_ref)] + raw_pairs
    pairs += [(tokens_at(key_hbm, n, T * GROUPS), raw_k.at[n]) for n in order]
    copies = start_copies(pairs, sems)
    wait_all(copies[:2])
    current = jnp.zeros((width, N), F32)
    sent = []
    for step, n in enumerate(order):
        copies[2 + step].wait()
        queries = own_group(raw_q[n], group_ref[0], all_q.at[step % 2])
        own_query_ref[n * T : (n + 1) * T, :] = queries
        sums, mid, last = chunk_logs(logs_ref, n)
        scaled = lanes_of(cot_ref, n).astype(F32) * rows(jnp.exp(sums - mid))
        scaled = jnp.where(live_mask(n, length_ref[0], width), scaled, 0.0)
        high, low = split(scaled)
        pulled = dot(side(high, low), twice(queries))
        ends_ref[n] = current
        sent += start_copies([(ends_ref.at[n], ends_hbm.at[n])], sems, len(copies) + step)
        current = rows(jnp.exp(last)) * current + rows(jnp.exp(mid)) * pulled
    start_ref[...] = current
    for step, n in enumerate(order):
        copies[2 + chunks + step].wait()
        own_key_ref[n * T : (n + 1) * T, :] = own_group(raw_k[n], group_ref[0], all_k.at[step % 2])
    pairs = [(own_key_ref, own_key_hbm), (own_query_ref, own_query_hbm)]
    wait_all(sent + start_copies(pairs, sems, len(copies) + chunks))


PLANES = 8


def half_rows(place, core):
    return pl.multiple_of((place // PLANES) * 8 * HEAD + core * 4 * HEAD + (place % PLANES) * PART, PART)


def summary_kernel(
    core_ref, input_hbm, cot_hbm, logs_hbm, key_hbm, query_hbm,
    carried_hbm, pulled_hbm, mine_ref, peer_ref, total_ref,
    input_ref, cot_ref, logs_ref, key_ref, query_ref, carried_ref, pulled_ref, all_c, all_p, sems,
):
    chunks = carried_ref.shape[0]
    order = range(chunks)
    pairs = [
        (logs_hbm, logs_ref), (key_hbm, key_ref), (input_hbm, input_ref), (query_hbm, query_ref), (cot_hbm, cot_ref)
    ]
    copies = start_copies(pairs, sems)
    wait_all(copies[:3])
    total = jnp.zeros(total_ref.shape, F32)
    sent = []
    for n in order:
        sums, mid, last = chunk_logs(logs_ref, n)
        high, low = split(lanes_of(input_ref, n).astype(F32) * rows(jnp.exp(mid - sums)))
        carried = dot(side(high, low), twice(tokens_of(key_ref, n)))
        carried = rows(jnp.exp(last - mid)) * carried
        carried_ref[n] = carried
        sent += start_copies([(carried_ref.at[n], carried_hbm.at[n])], sems, len(copies) + 2 * n)
        all_c[...] = carried if n == 0 else rows(jnp.exp(last)) * all_c[...] + carried
        if n == 0:
            wait_all(copies[3:])
        high, low = split(lanes_of(cot_ref, n).astype(F32) * rows(jnp.exp(sums - mid)))
        pulled = dot(side(high, low), twice(tokens_of(query_ref, n)))
        pulled = rows(jnp.exp(mid)) * pulled
        pulled_ref[n] = pulled
        sent += start_copies([(pulled_ref.at[n], pulled_hbm.at[n])], sems, len(copies) + 2 * n + 1)
        all_p[...] = pulled if n == 0 else all_p[...] + rows(jnp.exp(total)) * pulled
        total = total + last
    total_ref[...] = total
    core = core_ref[0]
    places = mine_ref.shape[0]
    for place in range(places):
        for ref, side_core in ((mine_ref, core), (peer_ref, 1 - core)):
            here = pl.ds(half_rows(place, side_core), PART)
            ref[place, :PART] = all_c[here, :]
            ref[place, PART:] = all_p[here, :]
    heads = total_ref.shape[0]
    peer_ref[places, :heads] = total_ref[...]
    peer_ref[places, heads:] = jnp.zeros_like(peer_ref[places, heads:])
    wait_all(sent)


def hold_kernel(mine_ref, total_ref, mine_out_ref, total_out_ref):
    mine_out_ref[...] = mine_ref[...]
    total_out_ref[...] = total_ref[...]


def both_totals(first, head, mine_ref, got_ref):
    mine = mine_ref[pl.ds(head, 1), :]
    theirs = got_ref[got_ref.shape[0] - 1, pl.ds(head, 1), :]
    return jnp.where(first, mine, theirs), jnp.where(first, theirs, mine)


STATES = 2 * PART
GRADS = STATES + 8


def head_of(place, side_y, core):
    return side_y * 8 + core * 4 + place * PART // HEAD


def joined(first, mine, theirs, total0, total1):
    zero, one = jnp.where(first, mine, theirs), jnp.where(first, theirs, mine)
    return jnp.exp(total1) * zero[:PART] + one[:PART], zero[PART:] + jnp.exp(total0) * one[PART:]


def parted(first, mine, theirs, total0, total1, start, end):
    carried0 = jnp.where(first, mine[:PART], theirs[:PART])
    pulled1 = jnp.where(first, theirs[PART:], mine[PART:])
    start1 = jnp.exp(total0) * start + carried0
    end0 = jnp.exp(total1) * end + pulled1
    own = jnp.where(first, start, start1), jnp.where(first, end0, end)
    return own, (jnp.where(first, start1, start), jnp.where(first, end, end0))


def pack_chip_kernel(at_ref, mine_ref, got_ref, total_ref, keep_ref, away_ref, chip_total_ref):
    core, y = at_ref[0], at_ref[1]
    heads = total_ref.shape[0]
    chip_total_ref[...] = total_ref[...] + got_ref[got_ref.shape[0] - 1, :heads]
    for place in range(PLANES):
        for ref, side_y in ((keep_ref, y), (away_ref, 1 - y)):
            total0, total1 = both_totals(core == 0, head_of(place, side_y, core), total_ref, got_ref)
            here = side_y * PLANES + place
            carried, pulled = joined(core == 0, mine_ref[here], got_ref[here], total0, total1)
            ref[place, :PART] = carried
            ref[place, PART:] = pulled
    away_ref[PLANES, :heads] = chip_total_ref[...]
    away_ref[PLANES, heads:] = jnp.zeros_like(away_ref[PLANES, heads:])


def pack_kernel(at_ref, keep_ref, got_ref, total_ref, start_ref, out_ref):
    core, y = at_ref[0], at_ref[1]
    for place in range(PLANES):
        total0, total1 = both_totals(y == 0, head_of(place, y, core), total_ref, got_ref)
        carried, pulled = joined(y == 0, keep_ref[place], got_ref[place], total0, total1)
        out_ref[place, :PART] = carried
        out_ref[place, PART:STATES] = pulled
        out_ref[place, STATES:GRADS] = jnp.broadcast_to(total0 + total1, (8, N))
        out_ref[place, GRADS:] = start_ref[PART * place : PART * (place + 1)]


def scan_kernel(blocks_ref, starts_ref, out_ref):
    current = jnp.zeros((PART, N), F32)
    for place in range(PLANES):
        starts_ref[place] = current
        current = jnp.exp(blocks_ref[place, STATES : STATES + 1]) * current + blocks_ref[place, :PART]
    for group in range(out_ref.shape[0]):
        out_ref[group, :PART] = blocks_ref[group, GRADS:]
        out_ref[group, PART:] = current


def scan_back_kernel(blocks_ref, starts_ref, got_ref, out_ref):
    current = got_ref[0, :PART]
    for answer in range(1, got_ref.shape[0]):
        current = current + got_ref[answer, :PART]
    for place in range(PLANES - 1, -1, -1):
        out_ref[place, :PART] = starts_ref[place]
        out_ref[place, PART:STATES] = current
        out_ref[place, STATES:] = got_ref[place, PART:]
        current = jnp.exp(blocks_ref[place, STATES : STATES + 1]) * current + blocks_ref[place, PART:STATES]


def unpack_kernel(at_ref, keep_ref, got_ref, total_ref, states_ref, own_ref, other_ref):
    core, y = at_ref[0], at_ref[1]
    for place in range(PLANES):
        total0, total1 = both_totals(y == 0, head_of(place, y, core), total_ref, got_ref)
        own, other = parted(
            y == 0, keep_ref[place], got_ref[place], total0, total1,
            states_ref[place, :PART], states_ref[place, PART:STATES],
        )
        for ref, (start, end) in ((own_ref, own), (other_ref, other)):
            ref[place, :PART] = start
            ref[place, PART:] = end


def unpack_chip_kernel(at_ref, mine_ref, got_ref, total_ref, near_ref, away_ref, own_ref, other_ref):
    core, y = at_ref[0], at_ref[1]
    for place in range(PLANES):
        for chip_ref, side_y in ((near_ref, y), (away_ref, 1 - y)):
            total0, total1 = both_totals(core == 0, head_of(place, side_y, core), total_ref, got_ref)
            here = side_y * PLANES + place
            own, other = parted(
                core == 0, mine_ref[here], got_ref[here], total0, total1,
                chip_ref[place, :PART], chip_ref[place, PART:],
            )
            for ref, (start, end) in ((own_ref, own), (other_ref, other)):
                ref[here, :PART] = start
                ref[here, PART:] = end


def gather_kernel(parts_ref, key_ref, query_ref, sums_ref):
    for ref, first in ((key_ref, 0), (query_ref, PART)):
        for group in range(GROUPS):
            chip0, chip1 = parts_ref[2 * group], parts_ref[2 * group + 1]
            sums_ref[pl.ds(group, PART, stride=GROUPS), :] = (chip0 + chip1)[first : first + PART]
        ref[...] = sums_ref[...].astype(BF16)


def chunk_grads(inputs, cot, logs3, keys, queries, start, end):
    sums, mid, last = logs3
    grow = rows(jnp.exp(mid - sums))
    fall = rows(jnp.exp(sums - mid))
    in_high, in_low = split(inputs * grow)
    cot_high, cot_low = split(cot * fall)
    end_high, end_low = split(rows(jnp.exp(last - mid)) * end)
    start_high, start_low = split(rows(jnp.exp(mid)) * start)
    first = lax.broadcasted_iota(jnp.int32, (T, T), 0)
    second = lax.broadcasted_iota(jnp.int32, (T, T), 1)
    score_high, score_low = split(jnp.where(first >= second, dot_nt(queries, keys), 0.0))
    input_grad = dot(side(cot_high, cot_low), twice(score_high)) + dot(cot_high, score_low)
    input_grad = input_grad + dot_nt(side(end_high, end_low), side(keys, keys))
    input_grad = grow * input_grad
    in_high_t, in_low_t = in_high.T, in_low.T
    right_high, right_low = side(cot_high, end_high), side(cot_low, end_low)
    both = dot(in_high_t, right_high) + (dot(in_high_t, right_low) + dot(in_low_t, right_high))
    products = jnp.where(second >= first, both[:, :T], 0.0)
    high, low = split(products)
    key_grad = both[:, T:] + dot(side(high, low), twice(queries))
    high, low = split(products.T)
    query_grad = dot(side(high, low), twice(keys))
    cot_high_t, cot_low_t = cot_high.T, cot_low.T
    query_grad = query_grad + dot(cot_high_t, start_high)
    query_grad = query_grad + (dot(cot_high_t, start_low) + dot(cot_low_t, start_high))
    return input_grad, key_grad, query_grad, (in_high, in_low)


def by_core(number, core, value, mine_ref, peer_ref):
    value = value.reshape(2, 2, PART, N)
    here = pl.ds(2 * number, 2)
    mine_ref[here] = jnp.where(core == 0, value[:, 0], value[:, 1])
    peer_ref[here] = jnp.where(core == 0, value[:, 1], value[:, 0])


def answer_kernel(
    length_ref, core_ref, input_hbm, cot_hbm, logs_hbm, key_hbm, query_hbm, ends_hbm,
    input_grad_hbm, query_grad_hbm, key_mine_ref, key_peer_ref,
    input_ref, cot_ref, logs_ref, key_ref, query_ref, ends_ref, input_grad_ref, query_grad_ref, state_ref, sems,
):
    chunks, width = ends_ref.shape[0], ends_ref.shape[1]
    order = range(chunks)
    pairs = [
        (logs_hbm, logs_ref), (key_hbm, key_ref), (query_hbm, query_ref), (input_hbm, input_ref), (cot_hbm, cot_ref)
    ]
    copies = start_copies(pairs + chunk_pairs(ends_hbm, ends_ref, order), sems)
    wait_all(copies[:5])
    state_ref[...] = jnp.zeros_like(state_ref)
    sent = []
    for n in order:
        logs3 = chunk_logs(logs_ref, n)
        sums, mid, last = logs3
        copies[5 + n].wait()
        cot = jnp.where(live_mask(n, length_ref[0], width), lanes_of(cot_ref, n).astype(F32), 0.0)
        keys, queries = tokens_of(key_ref, n), tokens_of(query_ref, n)
        start = state_ref[...]
        input_grad, key_grad, query_grad, (high, low) = chunk_grads(
            lanes_of(input_ref, n).astype(F32), cot, logs3, keys, queries, start, ends_ref[n]
        )
        input_grad_ref[n] = input_grad.astype(BF16)
        by_core(n, core_ref[0], key_grad, key_mine_ref, key_peer_ref)
        query_grad_ref[n * T : (n + 1) * T, :] = query_grad
        pairs = [
            (input_grad_ref.at[n], lanes_at(input_grad_hbm, n)),
            (tokens_at(query_grad_ref, n), tokens_at(query_grad_hbm, n)),
        ]
        sent += start_copies(pairs, sems, len(copies) + 2 * n)
        carried = dot(side(high, low), twice(keys))
        state_ref[...] = rows(jnp.exp(last)) * start + rows(jnp.exp(last - mid)) * carried
    wait_all(sent)


def prompt_near_kernel(
    input_hbm, cot_hbm, logs_hbm, key_hbm, query_hbm, input_grad_hbm, key_grad_hbm, query_grad_hbm,
    input_ref, cot_ref, logs_ref, key_ref, query_ref, input_grad_ref, key_grad_ref, query_grad_ref, sems,
):
    first = lax.broadcasted_iota(jnp.int32, (T, T), 0)
    second = lax.broadcasted_iota(jnp.int32, (T, T), 1)
    order = range(input_ref.shape[1] // T)
    pairs = [
        (logs_hbm, logs_ref), (key_hbm, key_ref), (query_hbm, query_ref), (input_hbm, input_ref), (cot_hbm, cot_ref)
    ]
    copies = start_copies(pairs, sems)
    wait_all(copies)
    sent = []
    for n in order:
        here = slice(n * T, (n + 1) * T)
        sums, mid, _ = chunk_logs(logs_ref, n)
        keys, queries = tokens_of(key_ref, n), tokens_of(query_ref, n)
        grow = rows(jnp.exp(mid - sums))
        in_high, in_low = split(lanes_of(input_ref, n).astype(F32) * grow)
        cot_high, cot_low = split(lanes_of(cot_ref, n).astype(F32) * rows(jnp.exp(sums - mid)))
        score_high, score_low = split(jnp.where(first >= second, dot_nt(queries, keys), 0.0))
        input_grad = dot(side(cot_high, cot_low), twice(score_high)) + dot(cot_high, score_low)
        input_grad_ref[n] = grow * input_grad
        in_high_t, in_low_t = in_high.T, in_low.T
        both = dot(in_high_t, side(cot_high, cot_low))
        products = both[:, :T] + (both[:, T:] + dot(in_low_t, cot_high))
        products = jnp.where(second >= first, products, 0.0)
        high, low = split(products)
        key_grad_ref[here, :] = dot(side(high, low), twice(queries))
        high, low = split(products.T)
        query_grad_ref[here, :] = dot(side(high, low), twice(keys))
        pairs = [
            (input_grad_ref.at[n], input_grad_hbm.at[n]),
            (tokens_at(key_grad_ref, n), tokens_at(key_grad_hbm, n)),
            (tokens_at(query_grad_ref, n), tokens_at(query_grad_hbm, n)),
        ]
        sent += start_copies(pairs, sems, len(copies) + 3 * n)
    wait_all(sent)


def prompt_far_kernel(
    core_ref, input_hbm, cot_hbm, logs_hbm, key_hbm, carried_hbm, pulled_hbm,
    near_input_hbm, near_key_hbm, near_query_hbm, own_hbm, got_hbm,
    input_grad_hbm, key_grad_hbm, query_grad_hbm,
    input_ref, cot_ref, logs_ref, key_ref, carried_ref, pulled_ref, near_input_ref, near_key_ref, near_query_ref,
    own_ref, got_ref, input_grad_ref, key_grad_ref, query_grad_ref, end_ref, start_ref, sems,
):
    chunks = carried_ref.shape[0]
    core = core_ref[0]
    order = range(chunks)
    pairs = [
        (own_hbm, own_ref), (got_hbm, got_ref), (logs_hbm, logs_ref), (key_hbm, key_ref), (input_hbm, input_ref),
        (cot_hbm, cot_ref), (near_key_hbm, near_key_ref), (near_query_hbm, near_query_ref),
    ]
    first = len(pairs)
    for three in zip(
        chunk_pairs(near_input_hbm, near_input_ref, order[::-1]), chunk_pairs(pulled_hbm, pulled_ref, order[::-1]),
        chunk_pairs(carried_hbm, carried_ref, order),
    ):
        pairs += three
    copies = start_copies(pairs, sems)
    wait_all(copies[:2])
    for place in range(own_ref.shape[0]):
        for ref, side_core in ((own_ref, core), (got_ref, 1 - core)):
            here = pl.ds(half_rows(place, side_core), PART)
            start_ref[here, :] = ref[place, :PART]
            end_ref[here, :] = ref[place, PART:]
    wait_all(copies[2:first])
    sent = []
    for step in range(chunks):
        wait_all(copies[first + 3 * step : first + 3 * step + 3])
        n = chunks - 1 - step
        here = slice(n * T, (n + 1) * T)
        sums, mid, last = chunk_logs(logs_ref, n)
        end = end_ref[...]
        end_ref[...] = rows(jnp.exp(last)) * end + pulled_ref[n]
        keys = tokens_of(key_ref, n)
        grow = rows(jnp.exp(mid - sums))
        in_high, in_low = split(lanes_of(input_ref, n).astype(F32) * grow)
        end_high, end_low = split(rows(jnp.exp(last - mid)) * end)
        input_grad = dot_nt(side(end_high, end_low), side(keys, keys))
        input_grad_ref[n] = (near_input_ref[n] + grow * input_grad).astype(BF16)
        pairs = [(input_grad_ref.at[n], lanes_at(input_grad_hbm, n))]
        sent += start_copies(pairs, sems, len(copies) + 3 * step)
        in_high_t, in_low_t = in_high.T, in_low.T
        both = dot(in_high_t, side(end_high, end_low))
        key_grad = both[:, :N] + (both[:, N:] + dot(in_low_t, end_high))
        key_grad_ref[here, :] = (near_key_ref[here, :] + key_grad).astype(BF16)
        pairs = [(tokens_at(key_grad_ref, n), tokens_at(key_grad_hbm, n))]
        sent += start_copies(pairs, sems, len(copies) + 3 * step + 1)

        n = step
        here = slice(n * T, (n + 1) * T)
        sums, mid, last = chunk_logs(logs_ref, n)
        start = start_ref[...]
        start_ref[...] = rows(jnp.exp(last)) * start + carried_ref[n]
        cot_high, cot_low = split(lanes_of(cot_ref, n).astype(F32) * rows(jnp.exp(sums - mid)))
        start_high, start_low = split(rows(jnp.exp(mid)) * start)
        cot_high_t, cot_low_t = cot_high.T, cot_low.T
        both = dot(cot_high_t, side(start_high, start_low))
        query_grad = both[:, :N] + (both[:, N:] + dot(cot_low_t, start_high))
        query_grad_ref[here, :] = (near_query_ref[here, :] + query_grad).astype(BF16)
        pairs = [(tokens_at(query_grad_ref, n), tokens_at(query_grad_hbm, n))]
        sent += start_copies(pairs, sems, len(copies) + 3 * step + 2)
    wait_all(sent)


def prepare_kernel(length_ref, cot_ref, logs_ref, local_ref, high_ref, low_ref, local_out_ref):
    local_out_ref[...] = local_ref[...]
    total = jnp.zeros((logs_ref.shape[0], T), F32)
    for n in range(cot_ref.shape[1] // T):
        sums, _, last = chunk_logs(logs_ref, n)
        scaled = lanes_of(cot_ref, n).astype(F32) * rows(jnp.exp(total + sums))
        scaled = jnp.where(live_mask(n, length_ref[0], cot_ref.shape[0]), scaled, 0.0)
        high, low = split(scaled)
        high_ref[n * T : (n + 1) * T, :] = high.T
        low_ref[n * T : (n + 1) * T, :] = low.T
        total = total + last


def start_part_kernel(core_ref, high_ref, low_ref, local_ref, state_ref, mine_ref, peer_ref):
    state = jnp.concatenate([state_ref[place, STATES:] for place in range(state_ref.shape[0])], axis=0)
    state_high, state_low = split(state)
    both = side(state_high, state_low)
    for n in range(high_ref.shape[0] // T):
        part = dot(tokens_of(high_ref, n), both)
        part = part[:, :N] + (part[:, N:] + dot(tokens_of(low_ref, n), state_high))
        by_core(n, core_ref[0], tokens_of(local_ref, n) + part, mine_ref, peer_ref)


def tail_kernel(key_ref, query_mine_ref, query_got_ref, out_ref):
    out_ref[:, :PART] = key_ref[...]
    out_ref[:, PART:] = query_mine_ref[...] + query_got_ref[...]


def shape(*dims, dtype=F32):
    return jax.ShapeDtypeStruct(dims, dtype)


IN_HBM = pl.BlockSpec(memory_space=pltpu.HBM)
IN_VMEM = pl.BlockSpec(memory_space=pltpu.VMEM)


def held(*dims, dtype=F32):
    return pltpu.VMEM(dims, dtype)


def loading(kernel, scalars, far, outs):
    def run(*refs):
        first, sources, rest = refs[:scalars], refs[scalars : scalars + far], refs[scalars + far :]
        *rest, sems = rest
        targets, rest = rest[len(rest) - far :], rest[: len(rest) - far]
        wait_all(start_copies(list(zip(sources, targets)), sems))
        kernel(*first, *targets, *rest)

    return run


def call(kernel, outs, scratch=(), copies=0, scalars=0, far=0, count=0, far_outs=0, flops=0, name=None):
    def run(*args):
        sems, extra, inner = copies, [], kernel
        if far and not copies:
            sources = args[scalars : scalars + far]
            extra = [pltpu.VMEM(source.shape, source.dtype) for source in sources]
            sems, inner = far, loading(kernel, scalars, far, outs)
        return pl.pallas_call(
            inner,
            out_shape=outs,
            in_specs=[pl.BlockSpec(memory_space=pltpu.SMEM)] * scalars + [IN_HBM] * far + [IN_VMEM] * count,
            out_specs=[IN_HBM] * far_outs + [IN_VMEM] * (len(outs) - far_outs),
            scratch_shapes=list(scratch) + extra + ([pltpu.SemaphoreType.DMA((sems,))] if sems else []),
            compiler_params=pltpu.CompilerParams(vmem_limit_bytes=LARGE if sems else SMALL),
            cost_estimate=pl.CostEstimate(flops=flops, bytes_accessed=2000000, transcendentals=0),
            name=name,
        )(*args)

    return run


def body(
    prompt_inputs, prompt_keys, prompt_queries, prompt_logdecay, prompt_cotangent,
    answer_inputs, answer_keys, answer_queries, answer_logdecay, answer_cotangent, answer_lengths,
):
    tokens, heads, _ = prompt_inputs.shape
    _, length, answer_heads, _ = answer_inputs.shape
    width, answer_width = heads * HEAD, answer_heads * HEAD
    chunks, answer_chunks = tokens // T, length // T
    seq, comp = lax.axis_size("seq"), lax.axis_size("comp")
    quads = heads // answer_heads
    planes = seq // quads
    chips = seq // 2
    same_core = [[2 * chip + side for chip in range(chips)] for side in range(2)]
    same_pair = [[quads * plane + q for plane in range(planes)] for q in range(quads)]
    place = lax.axis_index("seq").astype(jnp.int32)
    group = (place // quads).reshape(1)
    core, y = place % 2, place // 2 % 2
    at = jnp.stack([core, y])
    core = core.reshape(1)

    def swap_cores(value):
        return lax.ppermute(value, "seq", [(i, i ^ 1) for i in range(seq)])

    def swap_chips(value):
        return lax.ppermute(value, "seq", [(i, i ^ 2) for i in range(seq)])

    def over(value, axis, groups=None):
        return lax.all_to_all(value, axis, 0, 0, axis_index_groups=groups, tiled=True)

    x = jnp.transpose(prompt_inputs, (1, 2, 0)).reshape(width, tokens)
    cot = jnp.transpose(prompt_cotangent, (1, 2, 0)).reshape(width, tokens)
    logs = prompt_logdecay.T
    keys, queries = prompt_keys.reshape(tokens, N), prompt_queries.reshape(tokens, N)
    ax = jnp.transpose(answer_inputs[0], (1, 2, 0)).reshape(answer_width, length)
    acot = jnp.transpose(answer_cotangent[0], (1, 2, 0)).reshape(answer_width, length)
    alogs = answer_logdecay[0].T
    all_keys, all_queries = answer_keys.reshape(length * GROUPS, N), answer_queries.reshape(length * GROUPS, N)

    prompt_lanes, prompt_rows = held(width, tokens, dtype=BF16), held(tokens, N, dtype=BF16)
    prompt_states = held(chunks, width, N)
    prompt_scratch = [prompt_lanes, prompt_lanes, held(heads, tokens), prompt_rows, prompt_rows]
    carried, pulled, mine, peer, totals = call(
        summary_kernel,
        [
            shape(chunks, width, N), shape(chunks, width, N), shape(chips, 2 * PART, N),
            shape(chips + 1, 2 * PART, N), shape(heads, N),
        ],
        scratch=prompt_scratch + [prompt_states, prompt_states, held(width, N), held(width, N)],
        copies=5 + 2 * chunks, scalars=1, far=5, far_outs=2, flops=10**9, name="prompt_summary",
    )(core, x, cot, logs, keys, queries)
    theirs = swap_cores(peer)
    held_mine, held_totals = call(
        hold_kernel, [shape(chips, 2 * PART, N), shape(heads, N)], count=2, flops=10**7, name="hold"
    )(mine, totals)

    answer_lanes, answer_rows = held(answer_width, length, dtype=BF16), held(length, N, dtype=BF16)
    answer_logs, answer_states = held(answer_heads, length), held(answer_chunks, answer_width, N)
    raw, raw_chunk = held(answer_chunks, T * GROUPS, N, dtype=BF16), held(2, T * GROUPS, N)
    ends, akeys, aqueries, start_grad = call(
        ends_kernel,
        [
            shape(answer_chunks, answer_width, N), shape(length, N, dtype=BF16), shape(length, N, dtype=BF16),
            shape(answer_width, N),
        ],
        scratch=[answer_lanes, answer_logs, answer_states, answer_rows, answer_rows, raw, raw, raw_chunk, raw_chunk],
        copies=4 + 3 * answer_chunks, scalars=2, far=4, far_outs=3, flops=10**9, name="answer_ends",
    )(answer_lengths, group, acot, alogs, all_keys, all_queries)
    half = shape(planes, 2 * PART, N)
    half_more = shape(planes + 1, 2 * PART, N)
    keep, away, chip_totals = call(
        pack_chip_kernel, [half, half_more, shape(heads, N)], scalars=1, count=3, flops=10**7, name="pack_chip"
    )(at, held_mine, theirs, held_totals)
    chip_theirs = swap_chips(away)
    (sent,) = call(
        pack_kernel, [shape(planes, GRADS + PART, N)], scalars=1, count=4, flops=10**7, name="pack"
    )(at, keep, chip_theirs, chip_totals, start_grad)
    blocks = over(sent, "seq", same_pair)

    near_input, near_key, near_query = call(
        prompt_near_kernel, [shape(chunks, width, T), shape(tokens, N), shape(tokens, N)],
        scratch=prompt_scratch + [held(chunks, width, T), held(tokens, N), held(tokens, N)],
        copies=5 + 3 * chunks, far=5, far_outs=3, flops=3 * 10**9, name="prompt_near",
    )(x, cot, logs, keys, queries)
    ax_grad, aq_local, key_mine, key_peer = call(
        answer_kernel,
        [
            shape(answer_width, length, dtype=BF16), shape(length, N),
            shape(chips, PART, N), shape(chips, PART, N),
        ],
        scratch=[
            answer_lanes, answer_lanes, answer_logs, answer_rows, answer_rows, answer_states,
            held(answer_chunks, answer_width, T, dtype=BF16), held(length, N), held(answer_width, N),
        ],
        copies=5 + 3 * answer_chunks, scalars=2, far=6, far_outs=2, flops=3 * 10**9, name="answer_grads",
    )(answer_lengths, core, ax, acot, alogs, akeys, aqueries, ends)

    starts, sent = call(
        scan_kernel, [shape(planes, PART, N), shape(comp, 2 * PART, N)], count=1, flops=10**7, name="scan"
    )(blocks)
    sent, ax_grad, aq_local, key_mine, key_peer = lax.optimization_barrier(
        (sent, ax_grad, aq_local, key_mine, key_peer)
    )
    finals = over(sent, "comp")
    key_parts = key_mine + swap_cores(key_peer)
    finals, near_input, near_key, near_query, key_parts = lax.optimization_barrier(
        (finals, near_input, near_key, near_query, key_parts)
    )
    (sent,) = call(
        scan_back_kernel, [shape(planes, 3 * PART, N)], count=3, flops=10**7, name="scan_back"
    )(blocks, starts, finals)
    sent, late_cot, late_logs, aq_local = lax.optimization_barrier((sent, acot, alogs, aq_local))
    states = over(sent, "seq", same_pair)
    late_high, late_low, aq_local = call(
        prepare_kernel,
        [shape(length, answer_width, dtype=BF16), shape(length, answer_width, dtype=BF16), shape(length, N)],
        scalars=1, count=3, flops=10**9, name="answer_prepare",
    )(answer_lengths, late_cot, late_logs, aq_local)
    query_mine, query_peer = call(
        start_part_kernel, [shape(chips, PART, N), shape(chips, PART, N)],
        scalars=1, count=4, flops=10**9, name="answer_start_part",
    )(core, late_high, late_low, aq_local, states)
    states, query_mine, query_peer = lax.optimization_barrier((states, query_mine, query_peer))
    chip_own, chip_other = call(
        unpack_kernel, [half, half], scalars=1, count=4, flops=10**7, name="unpack"
    )(at, keep, chip_theirs, chip_totals, states)
    chip_got = swap_chips(chip_other)

    (sent,) = call(tail_kernel, [shape(chips, 2 * PART, N)], count=3, flops=10**7, name="pack_tail")(
        key_parts, query_mine, swap_cores(query_peer)
    )
    parts = over(sent, "seq", same_core)
    own, other = call(
        unpack_chip_kernel, [shape(chips, 2 * PART, N), shape(chips, 2 * PART, N)],
        scalars=1, count=5, flops=10**7, name="unpack_chip",
    )(at, mine, theirs, totals, chip_own, chip_got)
    x_grad, k_grad, q_grad = call(
        prompt_far_kernel,
        [shape(width, tokens, dtype=BF16), shape(tokens, N, dtype=BF16), shape(tokens, N, dtype=BF16)],
        scratch=[
            prompt_lanes, prompt_lanes, held(heads, tokens), prompt_rows, prompt_states, prompt_states,
            held(chunks, width, T), held(tokens, N), held(tokens, N),
            held(chips, 2 * PART, N), held(chips, 2 * PART, N),
            held(chunks, width, T, dtype=BF16), prompt_rows, prompt_rows, held(width, N), held(width, N),
        ],
        copies=8 + 6 * chunks, scalars=1, far=11, far_outs=3, flops=3 * 10**9, name="prompt_far",
    )(
        core, x, cot, logs, keys, carried, pulled, near_input, near_key, near_query, own, swap_cores(other),
    )

    parts, x_grad, k_grad, q_grad = lax.optimization_barrier((parts, x_grad, k_grad, q_grad))
    gathered = shape(PART * GROUPS, N, dtype=BF16)
    key_out, query_out = call(
        gather_kernel, [gathered, gathered], scratch=[held(PART * GROUPS, N)],
        count=1, flops=10**7, name="gather_groups",
    )(parts)

    return (
        jnp.transpose(x_grad.reshape(heads, HEAD, tokens), (2, 0, 1)),
        k_grad.reshape(tokens, 1, N),
        q_grad.reshape(tokens, 1, N),
        jnp.transpose(ax_grad.reshape(answer_heads, HEAD, length), (2, 0, 1))[None],
        key_out.reshape(1, PART, GROUPS, N),
        query_out.reshape(1, PART, GROUPS, N),
    )


def solution(mesh):
    in_specs = (
        P("seq", "comp", None),
        P("seq", "comp", None),
        P("seq", "comp", None),
        P("seq", "comp"),
        P("seq", "comp", None),
        P("comp", None, "seq", None),
        P("comp", None, None, None),
        P("comp", None, None, None),
        P("comp", None, "seq"),
        P("comp", None, "seq", None),
        P("comp"),
    )
    out_specs = (
        P("seq", "comp", None),
        P("seq", "comp", None),
        P("seq", "comp", None),
        P("comp", None, "seq", None),
        P("comp", "seq", None, None),
        P("comp", "seq", None, None),
    )
    return jax.shard_map(body, mesh=mesh, in_specs=in_specs, out_specs=out_specs, check_vma=False)
```
